32 devices in a mesh: lon: 8 (over z, core), lat: 4 (over y, x).
Axes of the slice: x: 2, y: 2, z: 4, core: 2. Of those that a mesh axis runs over, the one named last changes fastest.
Arguments:
- state: float32 [168, 64, 1024], P(None, 'lat', 'lon'), may hold values from -6 to 6
- noise: float32 [168, 64, 1024], P(None, 'lat', 'lon'), may hold values from -6 to 6
- first_kernel: bfloat16 [9, 256, 168], replicated, may hold values from -0.15625 to 0.15625
- middle_kernels: bfloat16 [2, 9, 256, 256], replicated, may hold values from -0.21875 to 0.21875
- last_kernel: bfloat16 [9, 168, 256], replicated, may hold values from -0.21875 to 0.21875
- obs_values: bfloat16 [768, 22, 128], P(('lon', 'lat')), may hold values from -6 to 6
- obs_holder: int32 [768, 1], P(('lon', 'lat')), may hold values from 0 to 31; in each aligned block of 24 rows (0 to 23, 24 to 47, ...) at most 2 rows name the same one
- obs_tile: int32 [768], P(('lon', 'lat')), may hold values from 0 to 15
- obs_operator: bfloat16 [22, 168], replicated, may hold values from -0.5 to 0.5
- obs_precision: float32 [22], replicated, may hold values from 0.3 to 3
- noise_level: float32 [1], replicated, may hold values from 0.25 to 1
- step_size: float32 [1], replicated, may hold values from 0.05 to 0.2
Outputs:
- state_next: float32 [168, 64, 1024], P(None, 'lat', 'lon')
The draws below stay inside these ranges and needn't reach their ends.
Inputs may be any that keep to these rules, and one draw needn't show every extreme that they name: `obs_holder`: the holder index counts lon-major: lon index times 4 plus lat index; the 24 blocks that one device holds (an aligned block of rows) name one holder at most 2 times, and exactly that often for some holder in every draw.
All inputs are finite; a program needn't handle non-finite values.
Results may differ from the reference program's by a relative error of at most 0.0095.
Values may be sent and summed in bfloat16 or wider, within the bound.
A program may use at most 128 MiB of HBM per device.

```python
import math
import jax
import jax.numpy as jnp
import numpy as np
from jax import lax

HIDDEN_SIZE = 256
LAYERS = 4
OBS_CHAN = 22
LAT_DEV = 16
LON_DEV = 128
CAPACITY = 2
CHANNELS = 168
BLOCK_DEV = 24
BLOCKS = 768
GRID_LAT = 64
GRID_LON = 1024
N_LON = 8
N_LAT = 4
DEVICES = 32


def place_ends(values, key, low, high):
    extent = values.shape
    index_at = [jax.random.randint(jax.random.fold_in(key, axis), (), 0, extent[axis]) for axis in range(len(extent))]
    values = values.at[tuple(index_at)].set(low)
    longest = extent.index(max(extent))
    index_at[longest] = (index_at[longest] + 1) % extent[longest]
    return values.at[tuple(index_at)].set(high)


def steps_of(key, extent, cuts, least, top_value):
    level = 1.0
    for axis_at, blocks in cuts:
        draws = jax.random.uniform(jax.random.fold_in(jax.random.fold_in(key, 6), axis_at), (blocks,), jnp.float32, least / len(cuts), top_value / len(cuts))
        level = level * jnp.repeat(jnp.exp(draws), extent[axis_at] // blocks).reshape((-1,) + (1,) * (len(extent) - 1 - axis_at))
    return level


def routed_block(key, own, number, rows, count, top, bound, skew):
    sequence = jax.random.permutation(key, count)
    heavy_load, common = portions_of(count, rows * top, bound, skew, True), portions_of(count, rows * top, bound, skew, False)
    places = jnp.arange(count)

    def named(lengths, rotation):
        used = int((lengths > 0).sum())
        fixed = max(1, used // 4)
        passed = fixed + (places - fixed + rotation * (used - fixed)) % max(1, count - fixed)
        return jnp.zeros((count,), jnp.int32).at[sequence[jnp.where(places < fixed, places, passed)]].set(jnp.asarray(lengths, jnp.int32))

    lengths = jnp.where(number % 4 == 0, named(heavy_load, number // 4), named(common, number - number // 4 - 1))
    mixed = jax.random.permutation(jax.random.fold_in(own, 3), count)
    source_of, taker = mixed[0:count // 2 * 2:2], mixed[1:count // 2 * 2:2]
    slack = jnp.minimum(lengths[source_of] - 1, bound - lengths[taker]) // 2
    slack = jnp.where((source_of == sequence[0]) | (taker == sequence[0]) | (lengths[taker] == 0), 0, jnp.maximum(slack, 0))
    passed = jax.random.randint(jax.random.fold_in(own, 4), (count // 2,), 0, 1 << 20) % (slack + 1)
    lengths = lengths.at[source_of].add(-passed).at[taker].add(passed)
    members = jnp.searchsorted(jnp.cumsum(lengths), jnp.arange(rows * top), side="right").astype(jnp.int32)
    grid = members.reshape(top, rows).T
    grid = grid[jax.random.permutation(jax.random.fold_in(own, 1), rows)]
    rotation = jax.random.randint(jax.random.fold_in(own, 2), (rows, 1), 0, top)
    return jnp.take_along_axis(grid, (jnp.arange(top)[None, :] + rotation) % top, axis=1)


def portions_of(amount, total, reach, lean, full):
    weights = [(1 << 20) // math.isqrt(standing ** lean) + 1 for standing in range(1, amount + 1)]
    largest = reach if full else min(reach, max(-(-total // amount), total * weights[0] // sum(weights)))
    least = 1 if total - largest >= amount - 1 else 0
    holding, surplus = [largest] + [least] * (amount - 1), total - largest - least * (amount - 1)
    while surplus > 0:
        free = [i for i in range(1, amount) if holding[i] < largest] or [i for i in range(1, amount) if holding[i] < reach]
        whole, budget = sum([weights[i] for i in free]), surplus
        for i in free:
            extra = min(reach - holding[i], max(1, budget * weights[i] // whole), surplus)
            holding[i] = holding[i] + extra
            surplus = surplus - extra
    return np.array(holding)


def centred(key, dims, scale, limit, shards=(), kind=jnp.bfloat16):
    values = scale * jax.random.normal(key, dims, jnp.float32)
    if shards:
        values = values * steps_of(key, dims, shards, -0.22, 0.18)
    return jnp.clip(values, -limit, limit).astype(kind)


def setup_inputs(seed: int = 0) -> dict:
    streams_of = jax.random.split(jax.random.key(seed), 13)
    state = centred(streams_of[0], (CHANNELS, GRID_LAT, GRID_LON), 1.0, 6.0, ((1, 4), (2, 8)), jnp.float32)
    noise = centred(streams_of[1], (CHANNELS, GRID_LAT, GRID_LON), 1.0, 6.0, ((1, 4), (2, 8)), jnp.float32)
    first_kernel = centred(streams_of[2], (9, HIDDEN_SIZE, CHANNELS), (9 * CHANNELS) ** -0.5, 0.15625)
    middle_kernels = centred(streams_of[3], (LAYERS - 2, 9, HIDDEN_SIZE, HIDDEN_SIZE), (3 * HIDDEN_SIZE) ** -0.5, 0.21875)
    last_kernel = centred(streams_of[4], (9, CHANNELS, HIDDEN_SIZE), (3 * HIDDEN_SIZE) ** -0.5, 0.21875)
    obs_values = centred(streams_of[5], (BLOCKS, OBS_CHAN, LON_DEV), 1.0, 6.0, ((0, 32),))
    obs_holder_keys = jax.random.split(jax.random.fold_in(streams_of[6], 1), BLOCKS // BLOCK_DEV)
    obs_holder_turns = jax.random.permutation(jax.random.fold_in(streams_of[6], 3), BLOCKS // BLOCK_DEV)
    obs_holder = jax.vmap(lambda own, number: routed_block(jax.random.fold_in(streams_of[6], 2), own, number, BLOCK_DEV, DEVICES, 1, CAPACITY, 2))(obs_holder_keys, obs_holder_turns).reshape((BLOCKS, 1))
    obs_tile = place_ends(jax.random.randint(streams_of[7], (BLOCKS,), 0, LAT_DEV), jax.random.fold_in(streams_of[7], 1), 0, LAT_DEV - 1).astype(jnp.int32)
    obs_operator = centred(streams_of[8], (OBS_CHAN, CHANNELS), CHANNELS ** -0.5, 0.5)
    obs_precision = jnp.clip(jnp.exp(jax.random.uniform(streams_of[9], (OBS_CHAN,), jnp.float32, math.log(0.3), math.log(3.0))), 0.3, 3.0)
    noise_level = jnp.clip(jnp.exp(jax.random.uniform(streams_of[10], (1,), jnp.float32, math.log(0.25), math.log(1.0))), 0.25, 1.0)
    step_size = jnp.clip(jnp.exp(jax.random.uniform(streams_of[11], (1,), jnp.float32, math.log(0.05), math.log(0.2))), 0.05, 0.2)
    return {"state": state, "noise": noise, "first_kernel": first_kernel, "middle_kernels": middle_kernels, "last_kernel": last_kernel, "obs_values": obs_values, "obs_holder": obs_holder, "obs_tile": obs_tile, "obs_operator": obs_operator, "obs_precision": obs_precision, "noise_level": noise_level, "step_size": step_size}


def pad_field(values_in):
    padded = jnp.pad(values_in, ((0, 0), (1, 1), (0, 0)))
    return jnp.concatenate([padded[:, :, -1:], padded, padded[:, :, :1]], axis=2)

def run_conv(padded, taps):
    result = lax.conv_general_dilated(padded.astype(jnp.float32)[None], taps, (1, 1), 'VALID', dimension_numbers=('NCHW', 'OIHW', 'NCHW'), precision=lax.Precision.HIGHEST)
    return result[0]

def forward_conv(padded, kernel):
    taps = kernel.astype(jnp.float32).reshape(3, 3, kernel.shape[1], kernel.shape[2])
    taps = jnp.transpose(taps, (2, 3, 0, 1))
    return run_conv(padded, taps)

def backward_conv(padded, kernel):
    taps = kernel.astype(jnp.float32).reshape(3, 3, kernel.shape[1], kernel.shape[2])
    taps = jnp.transpose(taps, (3, 2, 0, 1))[:, :, ::-1, ::-1]
    return run_conv(padded, taps)

def reference(state, noise, first_kernel, middle_kernels, last_kernel, obs_values, obs_holder, obs_tile, obs_operator, obs_precision, noise_level, step_size):
    kernels = [first_kernel] + [middle_kernels[index] for index in range(LAYERS - 2)] + [last_kernel]
    stored = []
    current = state.astype(jnp.bfloat16)
    for layer in range(LAYERS):
        outputs = forward_conv(pad_field(current), kernels[layer])
        stored.append(outputs)
        if layer + 1 < LAYERS:
            current = jax.nn.silu(outputs).astype(jnp.bfloat16)
    denoised = (state + stored[-1]).astype(jnp.bfloat16)
    holders = obs_holder[:, 0].reshape(DEVICES, BLOCK_DEV)
    tile_rows = obs_tile.reshape(DEVICES, BLOCK_DEV)
    grid_rows = (holders % N_LAT * LAT_DEV + tile_rows).astype(jnp.int32)
    grid_blocks = (holders // N_LAT).astype(jnp.int32)
    values = obs_values.reshape(DEVICES, BLOCK_DEV, OBS_CHAN, LON_DEV)
    blocked = denoised.reshape(CHANNELS, GRID_LAT, N_LON, LON_DEV)
    operator = obs_operator.astype(jnp.float32)

    def one_owner(carry, inputs):
        rows_here, blocks_here, values_here = inputs
        picked = blocked[:, rows_here, blocks_here, :].astype(jnp.float32)
        predicted = jnp.einsum('kc,cbl->bkl', operator, picked)
        weighted = ((values_here.astype(jnp.float32) - predicted) * obs_precision[None, :, None]).astype(jnp.bfloat16)
        contrib = jnp.einsum('kc,bkl->cbl', operator, weighted.astype(jnp.float32))
        return (carry.at[:, rows_here, blocks_here, :].add(contrib), None)
    start = jnp.zeros((CHANNELS, GRID_LAT, N_LON, LON_DEV), jnp.float32)
    pulled, unused = lax.scan(one_owner, start, (grid_rows, grid_blocks, values))
    pulled = pulled.reshape(CHANNELS, GRID_LAT, GRID_LON)
    cotangent = pulled.astype(jnp.bfloat16)
    back = pulled
    for layer in range(LAYERS - 1, -1, -1):
        back = backward_conv(pad_field(cotangent), kernels[layer])
        if layer > 0:
            sigmoid_in = jax.nn.sigmoid(stored[layer - 1])
            cotangent = (back * sigmoid_in * (1.0 + stored[layer - 1] * (1.0 - sigmoid_in))).astype(jnp.bfloat16)
    score = stored[-1] / (noise_level[0] * noise_level[0])
    return state + step_size[0] * (score + pulled + back) + jnp.sqrt(2.0 * step_size[0]) * noise
```

```python
import functools

import jax
import jax.numpy as jnp
from jax import lax
from jax.experimental import pallas as pl
from jax.experimental.pallas import tpu as pltpu
from jax.sharding import PartitionSpec as P

LAYERS = 4
CAPACITY = 2
MESH = pl.DeviceIdType.MESH
F32 = jnp.float32
BF16 = jnp.bfloat16
NT = (((1,), (1,)), ((), ()))
NN = (((1,), (0,)), ((), ()))


def mm(a, b, dims):
    return lax.dot_general(a, b, dims, preferred_element_type=F32)


def rows_padded(x, rows):
    extra = rows - x.shape[0]
    return jnp.concatenate([x, jnp.zeros((extra,) + x.shape[1:], x.dtype)], axis=0)


def corrector_kernel(
    n_lon,
    n_lat,
    rows,
    state_ref,
    w0_ref,
    wm_ref,
    w3_ref,
    op_ref,
    pv_ref,
    pc_ref,
    level_ref,
    out_ref,
    x_s,
    g_s,
    tot_s,
    w0p_s,
    w0t_s,
    w3p_s,
    opp_s,
    opt_s,
    edge_s,
    lon_s,
    lat_s,
    send_sem,
    recv_sem,
):
    width = 128
    hidden = w0_ref.shape[1]
    chans = w0_ref.shape[2]
    tall = (chans + 15) // 16 * 16
    obs = op_ref.shape[0]
    obs_rows = pv_ref.shape[1]
    lon, lat = lax.axis_index("lon"), lax.axis_index("lat")
    right, left = lax.rem(lon + 1, n_lon), lax.rem(lon + n_lon - 1, n_lon)
    down, up = lax.rem(lat + 1, n_lat), lax.rem(lat + n_lat - 1, n_lat)

    barrier = pltpu.get_barrier_semaphore()
    for where in ((right, lat), (left, lat), (lon, down), (lon, up)):
        pl.semaphore_signal(barrier, inc=1, device_id=where, device_id_type=MESH)
    pl.semaphore_wait(barrier, 4)

    def remote(src, dst, e, k, where):
        return pltpu.make_async_remote_copy(
            src_ref=src,
            dst_ref=dst,
            send_sem=send_sem.at[e, k],
            recv_sem=recv_sem.at[e, k],
            device_id=where,
            device_id_type=MESH,
        )

    def lat_copies(e):
        par = e % 2
        return (
            remote(x_s.at[par, 1, pl.ds(width, width)], lat_s.at[e, 1], e, 0, (lon, up)),
            remote(x_s.at[par, 1, pl.ds(rows * width, width)], lat_s.at[e, 0], e, 1, (lon, down)),
        )

    def lon_copies(e):
        return (
            remote(edge_s.at[e, 1], lon_s.at[e, 0], e, 2, (right, lat)),
            remote(edge_s.at[e, 0], lon_s.at[e, 1], e, 3, (left, lat)),
        )

    def put_row(e, row, act):
        par = e % 2
        span = pl.ds(pl.multiple_of((row + 1) * width, width), width)
        x_s[par, 1, span, :] = act.astype(BF16)
        x_s[par, 0, span, :] = pltpu.roll(act, 1, 0).astype(BF16)
        x_s[par, 2, span, :] = pltpu.roll(act, width - 1, 0).astype(BF16)
        edge_s[e, 0, pl.ds(row + 1, 1), :] = act[0:1, :]
        edge_s[e, 1, pl.ds(row + 1, 1), :] = act[width - 1 : width, :]

    def send_lat(e):
        for copy in lat_copies(e):
            copy.start()

    def finish_lat(e):
        for copy in lat_copies(e):
            copy.wait()
        top = jnp.where(lat == 0, 0.0, 1.0).astype(F32)
        bottom = jnp.where(lat == n_lat - 1, 0.0, 1.0).astype(F32)
        put_row(e, -1, lat_s[e, 0].astype(F32) * top)
        put_row(e, rows, lat_s[e, 1].astype(F32) * bottom)
        for copy in lon_copies(e):
            copy.start()

    def finish_lon(e):
        par = e % 2
        for copy in lon_copies(e):
            copy.wait()
        first = lax.broadcasted_iota(jnp.int32, (16, hidden), 0)

        def patch(r, carry):
            a = pl.ds(pl.multiple_of(r * width, width), 16)
            old = x_s[par, 0, a, :].astype(F32)
            x_s[par, 0, a, :] = jnp.where(first == 0, lon_s[e, 0, pl.ds(r, 1), :], old).astype(BF16)
            b = pl.ds(pl.multiple_of(r * width + width - 16, 16), 16)
            old = x_s[par, 2, b, :].astype(F32)
            x_s[par, 2, b, :] = jnp.where(first == 15, lon_s[e, 1, pl.ds(r, 1), :], old).astype(BF16)
            return carry

        lax.fori_loop(0, rows + 2, patch, 0)

    def window(e, r0, n, p, q):
        return x_s[e % 2, q, pl.ds(pl.multiple_of((r0 + p) * width, width), n * width), :]

    def all_rows(n, e, body):
        count = rows // n

        def ends(i, carry):
            body(i * (count - 1) * n)
            return carry

        def inner(i, carry):
            body((i + 1) * n)
            return carry

        lax.fori_loop(0, 2, ends, 0)
        if e is not None:
            send_lat(e)
        lax.fori_loop(0, count - 2, inner, 0)
        if e is not None:
            finish_lat(e)

    eye = (
        lax.broadcasted_iota(jnp.int32, (hidden, hidden), 0)
        == lax.broadcasted_iota(jnp.int32, (hidden, hidden), 1)
    ).astype(F32).astype(BF16)
    eye_w = eye[:width, :width]

    def state_row(r):
        return state_ref[pl.ds(r, chans, stride=rows), :]

    def turned(field):
        return mm(eye_w, rows_padded(field, hidden).astype(BF16), NT)

    edge_s[...] = jnp.zeros_like(edge_s)

    all_rows(2, 0, lambda r0: [put_row(0, r0 + i, turned(state_row(r0 + i))) for i in range(2)])

    w0p_s[...] = jnp.zeros_like(w0p_s)
    w3p_s[...] = jnp.zeros_like(w3p_s)
    opp_s[...] = jnp.zeros_like(opp_s)
    opp_s[0:obs, 0:chans] = op_ref[...].astype(F32)

    def weights(t, carry):
        w0p_s[t, :, 0:chans] = w0_ref[t]
        w3p_s[t, 0:chans, :] = w3_ref[t]
        w0t_s[t] = mm(eye, w0p_s[t], NT).astype(BF16)
        return carry

    lax.fori_loop(0, 9, weights, 0)
    opt_s[...] = mm(eye, opp_s[...].astype(BF16), NT).astype(BF16)

    taps = [lambda t: w0p_s[t], lambda t: wm_ref[0, t], lambda t: wm_ref[1, t], lambda t: w3p_s[t]]

    n = 4
    for layer in range(LAYERS - 1):
        finish_lon(layer)

        def forward(r0, layer=layer):
            pre = jnp.zeros((n * width, hidden), F32)
            for t in range(9):
                pre = pre + mm(window(layer, r0, n, t // 3, t % 3), taps[layer](t), NT)
            s = 0.5 * jnp.tanh(0.5 * pre) + 0.5
            act = pre * s
            g_s[layer, pl.ds(pl.multiple_of(r0 * width, width), n * width), :] = s * (
                1.0 + pre * (1.0 - s)
            )
            for i in range(n):
                put_row(layer + 1, r0 + i, act[i * width : (i + 1) * width])

        all_rows(n, layer + 1, forward)

    last = LAYERS - 1
    finish_lon(last)
    level = jnp.full((1, width), level_ref[0], F32)
    inverse = 1.0 / (level * level)

    def observe(r0):
        pre = jnp.zeros((tall, 2 * width), F32)
        for t in range(9):
            pre = pre + mm(w3p_s[t, 0:tall, :], window(last, r0, 2, t // 3, t % 3), NT)
        for i in range(2):
            row = r0 + i
            pre_row = pre[0:chans, i * width : (i + 1) * width]
            denoised = rows_padded(state_row(row) + pre_row, hidden).astype(BF16)
            predicted = mm(opp_s[0:obs_rows, :].astype(BF16), denoised, NN)
            weighted = pv_ref[row] - pc_ref[row] * predicted
            pulled = mm(opt_s[...], rows_padded(weighted, width).astype(BF16), NN)[0:chans, :]
            tot_s[row] = pre_row * inverse + pulled
            put_row(last + 1, row, turned(pulled))

    all_rows(2, last + 1, observe)

    for layer in range(LAYERS - 1, 0, -1):
        e = 2 * LAYERS - 1 - layer
        finish_lon(e)

        def backward(r0, layer=layer, e=e):
            back = jnp.zeros((n * width, hidden), F32)
            for t in range(9):
                back = back + mm(window(e, r0, n, 2 - t // 3, 2 - t % 3), taps[layer](t), NN)
            cot = back * g_s[layer - 1, pl.ds(pl.multiple_of(r0 * width, width), n * width), :]
            for i in range(n):
                put_row(e + 1, r0 + i, cot[i * width : (i + 1) * width])

        all_rows(n, e + 1, backward)

    e = 2 * LAYERS - 1
    finish_lon(e)

    def finish(r0):
        back = jnp.zeros((tall, 2 * width), F32)
        for t in range(9):
            back = back + mm(w0t_s[t, 0:tall, :], window(e, r0, 2, 2 - t // 3, 2 - t % 3), NT)
        for i in range(2):
            row = r0 + i
            total = tot_s[row] + back[0:chans, i * width : (i + 1) * width]
            out_ref[pl.ds(row, chans, stride=rows), :] = total

    all_rows(2, None, finish)


def corrector(state, w0, wm, w3, operator, pv, pc, level):
    chans, rows, width = state.shape
    hidden = w0.shape[1]
    exchanges = 2 * LAYERS
    edge_rows = (rows + 2 + 7) // 8 * 8
    cells = rows * width
    vmem = pl.BlockSpec(memory_space=pltpu.VMEM)
    flops = 2 * 9 * cells * 2 * (2 * hidden * hidden + 2 * hidden * chans)
    out = pl.pallas_call(
        functools.partial(
            corrector_kernel, lax.axis_size("lon"), lax.axis_size("lat"), rows
        ),
        out_shape=jax.ShapeDtypeStruct((chans * rows, width), F32),
        in_specs=[vmem] * 7 + [pl.BlockSpec(memory_space=pltpu.SMEM)],
        out_specs=vmem,
        scratch_shapes=[
            pltpu.VMEM((2, 3, (rows + 2) * width, hidden), BF16),
            pltpu.VMEM((LAYERS - 1, cells, hidden), F32),
            pltpu.VMEM((rows, chans, width), F32),
            pltpu.VMEM((9, hidden, hidden), BF16),
            pltpu.VMEM((9, hidden, hidden), BF16),
            pltpu.VMEM((9, hidden, hidden), BF16),
            pltpu.VMEM((width, hidden), F32),
            pltpu.VMEM((hidden, width), BF16),
            pltpu.VMEM((exchanges, 2, edge_rows, hidden), F32),
            pltpu.VMEM((exchanges, 2, edge_rows, hidden), F32),
            pltpu.VMEM((exchanges, 2, width, hidden), BF16),
            pltpu.SemaphoreType.DMA((exchanges, 4)),
            pltpu.SemaphoreType.DMA((exchanges, 4)),
        ],
        compiler_params=pltpu.CompilerParams(
            collective_id=0, has_side_effects=True, vmem_limit_bytes=56 * 1024 * 1024
        ),
        cost_estimate=pl.CostEstimate(flops=flops, bytes_accessed=8 * 1024 * 1024, transcendentals=0),
    )(state.reshape(chans * rows, width), w0, wm, w3, operator, pv, pc, level)
    return out.reshape(chans, rows, width)


def shards(
    state,
    noise,
    first_kernel,
    middle_kernels,
    last_kernel,
    obs_values,
    obs_holder,
    obs_tile,
    obs_operator,
    obs_precision,
    noise_level,
    step_size,
):
    row_count = state.shape[1]
    targets = obs_holder[:, 0]
    block_count = targets.shape[0]
    positions = lax.broadcasted_iota(jnp.int32, (block_count, block_count), 0)
    earlier = lax.broadcasted_iota(jnp.int32, (block_count, block_count), 1)
    before = (targets[:, None] == targets[None, :]) & (earlier < positions)
    ranks = jnp.sum(before.astype(jnp.int32), axis=1)
    slots = targets * CAPACITY + ranks
    slot_count = lax.axis_size(("lon", "lat")) * CAPACITY
    chosen = lax.broadcasted_iota(jnp.int32, (slot_count, block_count), 0) == slots[None, :]
    tile_send = jnp.max(jnp.where(chosen, obs_tile[None, :], -1), axis=1)
    flat = obs_values.reshape(block_count, -1)
    values_send = jnp.dot(chosen.astype(BF16), flat, preferred_element_type=F32).astype(BF16)
    values_send = values_send.reshape((slot_count,) + obs_values.shape[1:])
    values_recv = lax.all_to_all(values_send, ("lon", "lat"), split_axis=0, concat_axis=0, tiled=True)
    tile_recv = lax.all_to_all(tile_send, ("lon", "lat"), split_axis=0, concat_axis=0, tiled=True)
    onehot = (tile_recv[:, None] == lax.broadcasted_iota(jnp.int32, (1, row_count), 1)).astype(F32)
    summed = jnp.einsum(
        "sr,skl->rkl", onehot.astype(BF16), values_recv, preferred_element_type=F32
    )
    obs = obs_values.shape[1]
    padding = (obs + 15) // 16 * 16 - obs
    pv = jnp.pad(summed * obs_precision[None, :, None], ((0, 0), (0, padding), (0, 0)))
    pc = jnp.broadcast_to(
        jnp.sum(onehot, axis=0)[:, None, None] * obs_precision[None, :, None], summed.shape
    )
    pc = jnp.pad(pc, ((0, 0), (0, padding), (0, 0)))
    total = corrector(
        state, first_kernel, middle_kernels, last_kernel, obs_operator, pv, pc, noise_level
    )
    return state + step_size[0] * total + jnp.sqrt(2.0 * step_size[0]) * noise


def solution(mesh):
    placed = (
        P(None, "lat", "lon"),
        P(None, "lat", "lon"),
        P(),
        P(),
        P(),
        P(("lon", "lat"), None, None),
        P(("lon", "lat"), None),
        P(("lon", "lat")),
        P(),
        P(),
        P(),
        P(),
    )
    return jax.shard_map(
        shards, mesh=mesh, in_specs=placed, out_specs=P(None, "lat", "lon"), check_vma=False
    )
```

```python
import functools

import jax
import jax.numpy as jnp
from jax import lax
from jax.experimental import pallas as pl
from jax.experimental.pallas import tpu as pltpu
from jax.sharding import PartitionSpec as P

LAYERS = 4
CAPACITY = 2
MESH = pl.DeviceIdType.MESH
F32 = jnp.float32
BF16 = jnp.bfloat16
NT = (((1,), (1,)), ((), ()))
NN = (((1,), (0,)), ((), ()))


def mm(a, b, dims):
    return lax.dot_general(a, b, dims, preferred_element_type=F32)


def rows_padded(x, rows):
    extra = rows - x.shape[0]
    return jnp.concatenate([x, jnp.zeros((extra,) + x.shape[1:], x.dtype)], axis=0)


def corrector_kernel(
    n_lon,
    n_lat,
    rows,
    state_ref,
    w0_ref,
    wm_ref,
    w3_ref,
    op_ref,
    values_ref,
    place_ref,
    precision_ref,
    tile_ref,
    level_ref,
    out_ref,
    x_s,
    g_s,
    tot_s,
    wf_s,
    w0t_s,
    w3p_s,
    w3l_s,
    opp_s,
    opt_s,
    edge_s,
    lon_s,
    lat_s,
    block_s,
    route_s,
    first_s,
    second_s,
    pv_s,
    send_sem,
    recv_sem,
    first_send,
    first_recv,
    second_send,
    second_recv,
):
    width = 128
    hidden = w0_ref.shape[1]
    chans = w0_ref.shape[2]
    tall = (chans + 15) // 16 * 16
    obs = op_ref.shape[0]
    slot = pv_s.shape[1]
    pair = first_s.shape[2]
    lon, lat = lax.axis_index("lon"), lax.axis_index("lat")
    right, left = lax.rem(lon + 1, n_lon), lax.rem(lon + n_lon - 1, n_lon)
    down, up = lax.rem(lat + 1, n_lat), lax.rem(lat + n_lat - 1, n_lat)

    barrier = pltpu.get_barrier_semaphore()
    for k in range(1, n_lat):
        where = (lon, lax.rem(lat + k, n_lat))
        pl.semaphore_signal(barrier, inc=1, device_id=where, device_id_type=MESH)
    for k in range(1, n_lon):
        where = (lax.rem(lon + k, n_lon), lat)
        pl.semaphore_signal(barrier, inc=1, device_id=where, device_id_type=MESH)
    pl.semaphore_wait(barrier, n_lat + n_lon - 2)

    def remote(src, dst, ssem, rsem, where):
        return pltpu.make_async_remote_copy(
            src_ref=src,
            dst_ref=dst,
            send_sem=ssem,
            recv_sem=rsem,
            device_id=where,
            device_id_type=MESH,
        )

    def lat_copies(e):
        par = e % 2
        mid = pl.ds(hidden, hidden)
        return (
            remote(
                x_s.at[par, pl.ds(width, width), mid],
                lat_s.at[e, 1],
                send_sem.at[e, 0],
                recv_sem.at[e, 0],
                (lon, up),
            ),
            remote(
                x_s.at[par, pl.ds(rows * width, width), mid],
                lat_s.at[e, 0],
                send_sem.at[e, 1],
                recv_sem.at[e, 1],
                (lon, down),
            ),
        )

    def lon_copies(e):
        return (
            remote(
                edge_s.at[e, 1], lon_s.at[e, 0], send_sem.at[e, 2], recv_sem.at[e, 2], (right, lat)
            ),
            remote(
                edge_s.at[e, 0], lon_s.at[e, 1], send_sem.at[e, 3], recv_sem.at[e, 3], (left, lat)
            ),
        )

    def first_copies():
        return [
            remote(
                route_s.at[lax.rem(lat + k, n_lat)],
                first_s.at[lat],
                first_send.at[k],
                first_recv.at[k],
                (lon, lax.rem(lat + k, n_lat)),
            )
            for k in range(1, n_lat)
        ]

    def second_copies():
        return [
            remote(
                first_s.at[:, lax.rem(lon + k, n_lon)],
                second_s.at[lon],
                second_send.at[k],
                second_recv.at[k],
                (lax.rem(lon + k, n_lon), lat),
            )
            for k in range(1, n_lon)
        ]

    def part(e, q):
        return (q if e < LAYERS else 2 - q) * hidden

    def put_row(e, row, act):
        par = e % 2
        span = pl.ds(pl.multiple_of((row + 1) * width, width), width)
        x_s[par, span, pl.ds(hidden, hidden)] = act.astype(BF16)
        x_s[par, span, pl.ds(part(e, 0), hidden)] = pltpu.roll(act, 1, 0).astype(BF16)
        x_s[par, span, pl.ds(part(e, 2), hidden)] = pltpu.roll(act, width - 1, 0).astype(BF16)
        edge_s[e, 0, pl.ds(row + 1, 1), :] = act[0:1, :]
        edge_s[e, 1, pl.ds(row + 1, 1), :] = act[width - 1 : width, :]

    def send_lat(e):
        for copy in lat_copies(e):
            copy.start()

    def finish_lat(e):
        for copy in lat_copies(e):
            copy.wait()
        top = jnp.where(lat == 0, 0.0, 1.0).astype(F32)
        bottom = jnp.where(lat == n_lat - 1, 0.0, 1.0).astype(F32)
        put_row(e, -1, lat_s[e, 0].astype(F32) * top)
        put_row(e, rows, lat_s[e, 1].astype(F32) * bottom)
        for copy in lon_copies(e):
            copy.start()

    def finish_lon(e):
        par = e % 2
        for copy in lon_copies(e):
            copy.wait()
        first = lax.broadcasted_iota(jnp.int32, (16, hidden), 0)
        before, after = pl.ds(part(e, 0), hidden), pl.ds(part(e, 2), hidden)

        def patch(r, carry):
            a = pl.ds(pl.multiple_of(r * width, width), 16)
            old = x_s[par, a, before].astype(F32)
            new = jnp.where(first == 0, lon_s[e, 0, pl.ds(r, 1), :], old)
            x_s[par, a, before] = new.astype(BF16)
            b = pl.ds(pl.multiple_of(r * width + width - 16, 16), 16)
            old = x_s[par, b, after].astype(F32)
            new = jnp.where(first == 15, lon_s[e, 1, pl.ds(r, 1), :], old)
            x_s[par, b, after] = new.astype(BF16)
            return carry

        lax.fori_loop(0, rows + 2, patch, 0, unroll=2)

    def windows(e, r0, n):
        order = (0, 1, 2) if e < LAYERS else (2, 1, 0)
        return jnp.concatenate(
            [
                x_s[e % 2, pl.ds(pl.multiple_of((r0 + p) * width, width), n * width), :]
                for p in order
            ],
            axis=1,
        )

    def all_rows(n, e, body):
        count = rows // n

        def ends(i, carry):
            body(i * (count - 1) * n)
            return carry

        def inner(i, carry):
            body((i + 1) * n)
            return carry

        lax.fori_loop(0, 2, ends, 0)
        if e is not None:
            send_lat(e)
        lax.fori_loop(0, count - 2, inner, 0)
        if e is not None:
            finish_lat(e)

    eye = (
        lax.broadcasted_iota(jnp.int32, (hidden, hidden), 0)
        == lax.broadcasted_iota(jnp.int32, (hidden, hidden), 1)
    ).astype(F32).astype(BF16)
    eye_w = eye[:width, :width]

    def state_row(r):
        return state_ref[pl.ds(r, chans, stride=rows), :]

    def turned(field):
        return mm(eye_w, rows_padded(field, hidden).astype(BF16), NT)

    edge_s[...] = jnp.zeros_like(edge_s)

    all_rows(2, 0, lambda r0: [put_row(0, r0 + i, turned(state_row(r0 + i))) for i in range(2)])

    def tap(t):
        return pl.ds(pl.multiple_of(t * hidden, hidden), hidden)

    block_s[...] = jnp.zeros_like(block_s)

    def fill(b, carry):
        base = pl.multiple_of(b * slot, 8)
        block_s[pl.ds(base, obs), :] = values_ref[b].astype(F32)
        block_s[pl.ds(base + obs, 1), :] = jnp.full((1, width), tile_ref[b] + 1, jnp.int32).astype(F32)
        block_s[pl.ds(base + obs + 1, 1), :] = jnp.ones((1, width), F32)
        return carry

    lax.fori_loop(0, values_ref.shape[0], fill, 0)
    blocks = block_s[...].astype(BF16)
    per_lat = n_lon * pair

    def route(i, carry):
        ids = lax.broadcasted_iota(jnp.int32, (per_lat, blocks.shape[0]), 0) + i * per_lat
        chosen = (ids == place_ref[...]).astype(F32).astype(BF16)
        picked = mm(chosen, blocks, NN).astype(BF16)
        for j in range(n_lon):
            route_s[i, j] = picked[j * pair : (j + 1) * pair]
        return carry

    lax.fori_loop(0, n_lat, route, 0)
    for copy in first_copies():
        copy.start()
    first_s[lat] = route_s[lat]

    opp_s[...] = jnp.zeros_like(opp_s)
    opp_s[0:obs, 0:chans] = op_ref[...].astype(F32)
    w3p_s[...] = jnp.zeros_like(w3p_s)
    tot_s[...] = jnp.zeros_like(tot_s)

    def weights(t, carry):
        wide = rows_padded(w0_ref[t].astype(F32).T, hidden).astype(BF16)
        wf_s[0, tap(t), :] = wide
        w0t_s[:, tap(t)] = wide[0:tall]
        w3p_s[pl.ds(pl.multiple_of(t * hidden, hidden), chans), :] = w3_ref[t]
        w3l_s[:, tap(t)] = w3p_s[pl.ds(pl.multiple_of(t * hidden, hidden), tall), :]
        return carry

    lax.fori_loop(0, 9, weights, 0)
    opt_s[...] = mm(eye, opp_s[...].astype(BF16), NT).astype(BF16)

    def turn_middle(m):
        def one(t, carry):
            wf_s[m + 1, tap(t), :] = mm(eye, wm_ref[m, tap(t), :], NT).astype(BF16)
            return carry

        lax.fori_loop(0, 9, one, 0)

    n = 4
    for layer in range(LAYERS - 1):
        if layer >= 1:
            turn_middle(layer - 1)
        if layer == 1:
            for copy in first_copies():
                copy.wait()
            for copy in second_copies():
                copy.start()
            second_s[lon] = first_s[:, lon]
        finish_lon(layer)

        def forward(r0, layer=layer):
            pre = mm(windows(layer, r0, n), wf_s[layer], NN)
            s = 0.5 * jnp.tanh(0.5 * pre) + 0.5
            act = pre * s
            g_s[layer, pl.ds(pl.multiple_of(r0 * width, width), n * width), :] = s * (
                1.0 + pre * (1.0 - s)
            )
            for i in range(n):
                put_row(layer + 1, r0 + i, act[i * width : (i + 1) * width])

        all_rows(n, layer + 1, forward)

    for copy in second_copies():
        copy.wait()

    def gather(i, sums):
        both = second_s[i // n_lat, lax.rem(i, n_lat)].astype(F32)
        sums = list(sums)
        for j in range(CAPACITY):
            one = both[j * slot : (j + 1) * slot]
            ids = one[obs : obs + 1]
            for r in range(rows):
                sums[r] = sums[r] + jnp.where(ids == float(r + 1), one, 0.0)
        return tuple(sums)

    sums = lax.fori_loop(
        0, n_lon * n_lat, gather, tuple(jnp.zeros((slot, width), F32) for r in range(rows))
    )
    for r in range(rows):
        pv_s[r] = sums[r]
    diagonal = lax.broadcasted_iota(jnp.int32, (slot, obs), 0) == lax.broadcasted_iota(
        jnp.int32, (slot, obs), 1
    )
    precision = jnp.sum(
        jnp.where(diagonal, jnp.broadcast_to(precision_ref[...], (slot, obs)), 0.0),
        axis=1,
        keepdims=True,
    )

    last = LAYERS - 1
    finish_lon(last)
    level = jnp.full((1, width), level_ref[0], F32)
    inverse = 1.0 / (level * level)

    def observe(r0):
        pre = mm(w3l_s[...], windows(last, r0, 2), NT)
        for i in range(2):
            row = r0 + i
            pre_row = pre[0:chans, i * width : (i + 1) * width]
            denoised = rows_padded(state_row(row) + pre_row, hidden).astype(BF16)
            predicted = mm(opp_s[...].astype(BF16), denoised, NN)[0:slot]
            given = pv_s[row]
            weighted = (given - given[obs + 1 : obs + 2] * predicted) * precision
            pulled = mm(opt_s[...], rows_padded(weighted, width).astype(BF16), NN)[0:chans, :]
            tot_s[row] = pre_row * inverse + pulled
            put_row(last + 1, row, turned(pulled))

    all_rows(2, last + 1, observe)

    for layer in range(LAYERS - 1, 0, -1):
        e = 2 * LAYERS - 1 - layer
        finish_lon(e)

        def backward(r0, layer=layer, e=e):
            taps = w3p_s[...] if layer == LAYERS - 1 else wm_ref[layer - 1]
            back = mm(windows(e, r0, n), taps, NN)
            cot = back * g_s[layer - 1, pl.ds(pl.multiple_of(r0 * width, width), n * width), :]
            for i in range(n):
                put_row(e + 1, r0 + i, cot[i * width : (i + 1) * width])

        all_rows(n, e + 1, backward)

    e = 2 * LAYERS - 1
    finish_lon(e)

    def finish(r0):
        back = mm(w0t_s[...], windows(e, r0, 2), NT)
        for i in range(2):
            row = r0 + i
            total = tot_s[row] + back[0:chans, i * width : (i + 1) * width]
            out_ref[pl.ds(row, chans, stride=rows), :] = total

    all_rows(2, None, finish)


def corrector(state, w0, wm, w3, operator, values, place, precision, tile, level):
    chans, rows, width = state.shape
    hidden = w0.shape[1]
    tall = (chans + 15) // 16 * 16
    exchanges = 2 * LAYERS
    edge_rows = (rows + 2 + 7) // 8 * 8
    cells = rows * width
    slot = values.shape[1] + 2
    pair = CAPACITY * slot
    n_lon, n_lat = lax.axis_size("lon"), lax.axis_size("lat")
    vmem = pl.BlockSpec(memory_space=pltpu.VMEM)
    smem = pl.BlockSpec(memory_space=pltpu.SMEM)
    flops = 2 * 9 * cells * 2 * (2 * hidden * hidden + 2 * hidden * chans)
    out = pl.pallas_call(
        functools.partial(corrector_kernel, n_lon, n_lat, rows),
        out_shape=jax.ShapeDtypeStruct((chans * rows, width), F32),
        in_specs=[vmem] * 8 + [smem] * 2,
        out_specs=vmem,
        scratch_shapes=[
            pltpu.VMEM((2, (rows + 2) * width, 3 * hidden), BF16),
            pltpu.VMEM((LAYERS - 1, cells, hidden), F32),
            pltpu.VMEM((rows, chans, width), F32),
            pltpu.VMEM((LAYERS - 1, 9 * hidden, hidden), BF16),
            pltpu.VMEM((tall, 9 * hidden), BF16),
            pltpu.VMEM((9 * hidden, hidden), BF16),
            pltpu.VMEM((tall, 9 * hidden), BF16),
            pltpu.VMEM((width, hidden), F32),
            pltpu.VMEM((hidden, width), BF16),
            pltpu.VMEM((exchanges, 2, edge_rows, hidden), F32),
            pltpu.VMEM((exchanges, 2, edge_rows, hidden), F32),
            pltpu.VMEM((exchanges, 2, width, hidden), BF16),
            pltpu.VMEM((place.shape[1], width), F32),
            pltpu.VMEM((n_lat, n_lon, pair, width), BF16),
            pltpu.VMEM((n_lat, n_lon, pair, width), BF16),
            pltpu.VMEM((n_lon, n_lat, pair, width), BF16),
            pltpu.VMEM((rows, slot, width), F32),
            pltpu.SemaphoreType.DMA((exchanges, 4)),
            pltpu.SemaphoreType.DMA((exchanges, 4)),
            pltpu.SemaphoreType.DMA((n_lat,)),
            pltpu.SemaphoreType.DMA((n_lat,)),
            pltpu.SemaphoreType.DMA((n_lon,)),
            pltpu.SemaphoreType.DMA((n_lon,)),
        ],
        compiler_params=pltpu.CompilerParams(
            collective_id=0, has_side_effects=True, vmem_limit_bytes=56 * 1024 * 1024
        ),
        cost_estimate=pl.CostEstimate(flops=flops, bytes_accessed=8 * 1024 * 1024, transcendentals=0),
    )(
        state.reshape(chans * rows, width),
        w0,
        wm.reshape(wm.shape[0], 9 * hidden, hidden),
        w3,
        operator,
        values,
        place,
        precision[None, :],
        tile,
        level,
    )
    return out.reshape(chans, rows, width)


def shards(
    state,
    noise,
    first_kernel,
    middle_kernels,
    last_kernel,
    obs_values,
    obs_holder,
    obs_tile,
    obs_operator,
    obs_precision,
    noise_level,
    step_size,
):
    block_count, obs, width = obs_values.shape
    n_lon, n_lat = lax.axis_size("lon"), lax.axis_size("lat")
    slot = obs + 2
    depth = (block_count * slot + 127) // 128 * 128
    lane = lax.broadcasted_iota(jnp.int32, (1, depth), 1)
    owner = lane // slot
    targets = obs_holder
    listed = lax.broadcasted_iota(jnp.int32, (block_count, 1), 0)
    mine = jnp.sum(jnp.where(owner == listed, targets, 0), axis=0, keepdims=True)
    rank = jnp.sum(
        ((targets == mine) & (listed < owner)).astype(jnp.int32), axis=0, keepdims=True
    )
    place = ((mine % n_lat) * n_lon + mine // n_lat) * CAPACITY + rank
    place = jnp.where(owner < block_count, place * slot + lane % slot, -1)
    total = corrector(
        state,
        first_kernel,
        middle_kernels,
        last_kernel,
        obs_operator,
        obs_values,
        place,
        obs_precision,
        obs_tile,
        noise_level,
    )
    return state + step_size[0] * total + jnp.sqrt(2.0 * step_size[0]) * noise


def solution(mesh):
    placed = (
        P(None, "lat", "lon"),
        P(None, "lat", "lon"),
        P(),
        P(),
        P(),
        P(("lon", "lat"), None, None),
        P(("lon", "lat"), None),
        P(("lon", "lat")),
        P(),
        P(),
        P(),
        P(),
    )
    return jax.shard_map(
        shards, mesh=mesh, in_specs=placed, out_specs=P(None, "lat", "lon"), check_vma=False
    )
```

```python
import functools

import jax
import jax.numpy as jnp
from jax import lax
from jax.experimental import pallas as pl
from jax.experimental.pallas import tpu as pltpu
from jax.sharding import PartitionSpec as P

LAYERS = 4
CAPACITY = 2
MESH = pl.DeviceIdType.MESH
F32 = jnp.float32
BF16 = jnp.bfloat16
NT = (((1,), (1,)), ((), ()))
NN = (((1,), (0,)), ((), ()))


def mm(a, b, dims):
    return lax.dot_general(a, b, dims, preferred_element_type=F32)


def rows_padded(x, rows):
    extra = rows - x.shape[0]
    return jnp.concatenate([x, jnp.zeros((extra,) + x.shape[1:], x.dtype)], axis=0)


def corrector_kernel(
    n_lon,
    n_lat,
    rows,
    state_ref,
    w0_ref,
    wm_ref,
    w3_ref,
    op_ref,
    values_ref,
    place_ref,
    precision_ref,
    tile_ref,
    level_ref,
    step_ref,
    out_ref,
    xa_s,
    xb_s,
    g_s,
    state_s,
    tot_s,
    wf_s,
    w0p_s,
    w3p_s,
    opp_s,
    opt_s,
    edge_s,
    lon_s,
    lat_s,
    block_s,
    route_s,
    first_s,
    second_s,
    pv_s,
    count_s,
    precision_s,
    send_sem,
    recv_sem,
    first_send,
    first_recv,
    second_send,
    second_recv,
):
    width = 128
    hidden = w0_ref.shape[2]
    chans = w0_ref.shape[1]
    obs = op_ref.shape[0]
    slot = obs + 2
    x_s = (xa_s, xb_s)
    quarter = rows // 4
    ends = [0, rows - 1]
    near = list(range(1, quarter)) + list(range(rows - quarter + 1, rows - 1))
    middle = [quarter, quarter + 1, rows - quarter - 1, rows - quarter]
    far = list(range(quarter + 2, rows - quarter - 1))
    early = [r for r in range(-1, rows + 1) if r not in far]
    early_rows = (len(early) + 7) // 8 * 8
    late_rows = (len(far) + 7) // 8 * 8

    def at_edge(row):
        return early.index(row) if row in early else early_rows + far.index(row)

    pair = first_s.shape[2]
    lon, lat = lax.axis_index("lon"), lax.axis_index("lat")
    right, left = lax.rem(lon + 1, n_lon), lax.rem(lon + n_lon - 1, n_lon)
    down, up = lax.rem(lat + 1, n_lat), lax.rem(lat + n_lat - 1, n_lat)

    barrier = pltpu.get_barrier_semaphore()
    for k in range(1, n_lat):
        where = (lon, lax.rem(lat + k, n_lat))
        pl.semaphore_signal(barrier, inc=1, device_id=where, device_id_type=MESH)
    for k in range(1, n_lon):
        where = (lax.rem(lon + k, n_lon), lat)
        pl.semaphore_signal(barrier, inc=1, device_id=where, device_id_type=MESH)
    pl.semaphore_wait(barrier, n_lat + n_lon - 2)

    def remote(src, dst, ssem, rsem, where):
        return pltpu.make_async_remote_copy(
            src_ref=src,
            dst_ref=dst,
            send_sem=ssem,
            recv_sem=rsem,
            device_id=where,
            device_id_type=MESH,
        )

    def lat_copies(e):
        x = x_s[e % 2]
        mid = pl.ds(hidden, hidden)
        return (
            remote(
                x.at[pl.ds(width, width), mid],
                lat_s.at[e, 1],
                send_sem.at[e, 0],
                recv_sem.at[e, 0],
                (lon, up),
            ),
            remote(
                x.at[pl.ds(rows * width, width), mid],
                lat_s.at[e, 0],
                send_sem.at[e, 1],
                recv_sem.at[e, 1],
                (lon, down),
            ),
        )

    def lon_copies(e, late):
        span = pl.ds(early_rows, late_rows) if late else pl.ds(0, early_rows)
        k = 4 if late else 2
        return (
            remote(
                edge_s.at[e, 1, span],
                lon_s.at[e, 0, span],
                send_sem.at[e, k],
                recv_sem.at[e, k],
                (right, lat),
            ),
            remote(
                edge_s.at[e, 0, span],
                lon_s.at[e, 1, span],
                send_sem.at[e, k + 1],
                recv_sem.at[e, k + 1],
                (left, lat),
            ),
        )

    def first_copies():
        return [
            remote(
                route_s.at[lax.rem(lat + k, n_lat)],
                first_s.at[lat],
                first_send.at[k],
                first_recv.at[k],
                (lon, lax.rem(lat + k, n_lat)),
            )
            for k in range(1, n_lat)
        ]

    def second_copies():
        return [
            remote(
                first_s.at[:, lax.rem(lon + k, n_lon)],
                second_s.at[lon],
                second_send.at[k],
                second_recv.at[k],
                (lax.rem(lon + k, n_lon), lat),
            )
            for k in range(1, n_lon)
        ]

    def part(e, q):
        return (q if e < LAYERS else 2 - q) * hidden

    def span_of(row):
        return pl.ds((row + 1) * width, width)

    def put_row(e, row, act):
        x = x_s[e % 2]
        span = span_of(row)
        x[span, pl.ds(hidden, hidden)] = act.astype(BF16)
        x[span, pl.ds(part(e, 0), hidden)] = pltpu.roll(act, 1, 0).astype(BF16)
        x[span, pl.ds(part(e, 2), hidden)] = pltpu.roll(act, width - 1, 0).astype(BF16)
        edge_s[e, 0, pl.ds(at_edge(row), 1), :] = act[0:1, :]
        edge_s[e, 1, pl.ds(at_edge(row), 1), :] = act[width - 1 : width, :]

    def start(copies):
        for copy in copies:
            copy.start()

    def finish_lat(e):
        for copy in lat_copies(e):
            copy.wait()
        top = jnp.where(lat == 0, 0.0, 1.0).astype(F32)
        bottom = jnp.where(lat == n_lat - 1, 0.0, 1.0).astype(F32)
        put_row(e, -1, lat_s[e, 0].astype(F32) * top)
        put_row(e, rows, lat_s[e, 1].astype(F32) * bottom)

    def finish_lon(e, late):
        x = x_s[e % 2]
        for copy in lon_copies(e, late):
            copy.wait()
        first = lax.broadcasted_iota(jnp.int32, (16, hidden), 0)
        before, after = pl.ds(part(e, 0), hidden), pl.ds(part(e, 2), hidden)
        for row in far if late else early:
            spot = pl.ds(at_edge(row), 1)
            a = pl.ds((row + 1) * width, 16)
            x[a, before] = jnp.where(
                first == 0, lon_s[e, 0, spot, :], x[a, before].astype(F32)
            ).astype(BF16)
            b = pl.ds((row + 2) * width - 16, 16)
            x[b, after] = jnp.where(
                first == 15, lon_s[e, 1, spot, :], x[b, after].astype(F32)
            ).astype(BF16)

    def windows(e, group):
        order = (0, 1, 2) if e < LAYERS else (2, 1, 0)
        x = x_s[e % 2]
        return jnp.concatenate(
            [
                jnp.concatenate([x[span_of(row + p - 1), :] for row in group], axis=0)
                for p in order
            ],
            axis=1,
        )

    def layer_pass(e, body):
        sends = e + 1 < 2 * LAYERS
        finish_lon(e, False)
        body(ends)
        if sends:
            start(lat_copies(e + 1))
        body(near)
        finish_lon(e, True)
        body(middle)
        if sends:
            finish_lat(e + 1)
            start(lon_copies(e + 1, False))
        body(far)
        if sends:
            start(lon_copies(e + 1, True))

    eye = (
        lax.broadcasted_iota(jnp.int32, (hidden, hidden), 0)
        == lax.broadcasted_iota(jnp.int32, (hidden, hidden), 1)
    ).astype(F32).astype(BF16)

    edge_s[...] = jnp.zeros_like(edge_s)

    def load_row(row):
        field = state_ref[pl.ds(row, chans, stride=rows), :]
        turned = rows_padded(field, hidden).T
        state_s[pl.ds(row * width, width), :] = turned
        put_row(0, row, turned)

    for row in ends:
        load_row(row)
    start(lat_copies(0))
    for row in range(1, rows - 1):
        load_row(row)

    def tap(t):
        return pl.ds(pl.multiple_of(t * hidden, hidden), hidden)

    count = tile_ref.shape[0]
    block_s[...] = jnp.zeros_like(block_s)
    block_s[0 : obs * count, :] = values_ref[...].astype(F32)

    def fill(b, carry):
        number = jnp.full((1, width), tile_ref[b] + 1, jnp.int32).astype(F32)
        block_s[pl.ds(obs * count + b, 1), :] = number
        return carry

    lax.fori_loop(0, count, fill, 0)
    block_s[(obs + 1) * count : slot * count, :] = jnp.ones((count, width), F32)
    blocks = block_s[...].astype(BF16)
    per_lat = n_lon * pair

    def route(i, carry):
        ids = lax.broadcasted_iota(jnp.int32, (per_lat, blocks.shape[0]), 0) + i * per_lat
        chosen = (ids == place_ref[...]).astype(F32).astype(BF16)
        picked = mm(chosen, blocks, NN).astype(BF16)
        for j in range(n_lon):
            route_s[i, j] = picked[j * pair : (j + 1) * pair]
        return carry

    lax.fori_loop(0, n_lat, route, 0)
    start(first_copies())
    first_s[lat] = route_s[lat]
    finish_lat(0)
    start(lon_copies(0, False))
    start(lon_copies(0, True))

    opp_s[...] = jnp.zeros_like(opp_s)
    opp_s[0:obs, 0:chans] = op_ref[...].astype(F32)
    precision_s[...] = jnp.zeros_like(precision_s)
    precision_s[0:1, 0:obs] = precision_ref[...]
    wf_s[0] = jnp.zeros_like(wf_s[0])
    w3p_s[...] = jnp.zeros_like(w3p_s)
    for t in range(9):
        wf_s[0, t * hidden : t * hidden + chans, :] = w0_ref[t]
        w3p_s[t * hidden : t * hidden + chans, :] = w3_ref[t]

    def turn(dst, src):
        def one(t, carry):
            dst[tap(t), :] = mm(eye, src[tap(t), :], NT).astype(BF16)
            return carry

        lax.fori_loop(0, 9, one, 0)

    def turn_ahead(layer):
        if layer == 0:
            opt_s[...] = mm(eye, opp_s[...].astype(BF16), NT).astype(BF16)
            turn(wf_s.at[1], wm_ref.at[0])
        if layer == 1:
            turn(wf_s.at[2], wm_ref.at[1])
        if layer == 2:
            turn(wf_s.at[3], w3p_s)

    def cells_of(group):
        return [pl.ds(row * width, width) for row in group]

    def pick(ref, group):
        return jnp.concatenate([ref[span, :] for span in cells_of(group)], axis=0)

    def cells(field, i):
        return field[i * width : (i + 1) * width]

    for layer in range(LAYERS - 1):
        turn_ahead(layer)
        if layer == 1:
            for copy in first_copies():
                copy.wait()
            start(second_copies())
            second_s[lon] = first_s[:, lon]

        def forward(group, layer=layer):
            pre = mm(windows(layer, group), wf_s[layer], NN)
            s = 0.5 * jnp.tanh(0.5 * pre) + 0.5
            act = pre * s
            slope = (s * (1.0 + pre * (1.0 - s))).astype(BF16)
            for i, span in enumerate(cells_of(group)):
                g_s[layer, span, :] = cells(slope, i)
                put_row(layer + 1, group[i], cells(act, i))

        layer_pass(layer, forward)

    for copy in second_copies():
        copy.wait()

    def gather(i, sums):
        both = second_s[i // n_lat, lax.rem(i, n_lat)].astype(F32)
        sums = list(sums)
        for j in range(CAPACITY):
            one = both[j * slot : (j + 1) * slot]
            ids = one[obs : obs + 1]
            for r in range(rows):
                sums[r] = sums[r] + jnp.where(ids == float(r + 1), one, 0.0)
        return tuple(sums)

    sums = lax.fori_loop(
        0, n_lon * n_lat, gather, tuple(jnp.zeros((slot, width), F32) for r in range(rows))
    )
    precision = precision_s[0:1, :]
    for r in range(rows):
        pv_s[pl.ds(r * width, width), :] = rows_padded(sums[r], width).T * precision
        count_s[r : r + 1, :] = sums[r][obs + 1 : obs + 2, :] * precision

    last = LAYERS - 1
    level = jnp.full((1, hidden), level_ref[0], F32)
    inverse = 1.0 / (level * level)

    def observe(group):
        pre = mm(windows(last, group), wf_s[last], NN)
        denoised = (pick(state_s, group) + pre).astype(BF16)
        predicted = mm(denoised, opt_s[...], NN)
        weighted = jnp.concatenate(
            [
                pv_s[span, :] - count_s[row : row + 1, :] * cells(predicted, i)
                for i, (row, span) in enumerate(zip(group, cells_of(group)))
            ],
            axis=0,
        )
        pulled = mm(weighted.astype(BF16), opp_s[...].astype(BF16), NN)
        total = pre * inverse + pulled
        for i, span in enumerate(cells_of(group)):
            tot_s[span, :] = cells(total, i)
            put_row(last + 1, group[i], cells(pulled, i))

    layer_pass(last, observe)
    turn(w0p_s, wf_s.at[0])

    for layer in range(LAYERS - 1, 0, -1):
        e = 2 * LAYERS - 1 - layer

        def backward(group, layer=layer, e=e):
            taps = w3p_s[...] if layer == LAYERS - 1 else wm_ref[layer - 1]
            back = mm(windows(e, group), taps, NN)
            for i, span in enumerate(cells_of(group)):
                cot = cells(back, i) * g_s[layer - 1, span, :].astype(F32)
                put_row(e + 1, group[i], cot)

        layer_pass(e, backward)

    e = 2 * LAYERS - 1
    step = jnp.full((1, width), step_ref[0], F32)

    def finish(group):
        total = pick(tot_s, group) + mm(windows(e, group), w0p_s[...], NN)
        for i, row in enumerate(group):
            out_ref[pl.ds(row, chans, stride=rows), :] = cells(total, i).T[0:chans] * step

    layer_pass(e, finish)


def corrector(state, w0, wm, w3, operator, values, place, precision, tile, level, step):
    chans, rows, width = state.shape
    hidden = w0.shape[2]
    exchanges = 2 * LAYERS
    far = rows // 2 - 3
    edge_rows = (rows + 2 - far + 7) // 8 * 8 + (far + 7) // 8 * 8
    cells = rows * width
    slot = values.shape[0] + 2
    pair = CAPACITY * slot
    n_lon, n_lat = lax.axis_size("lon"), lax.axis_size("lat")
    vmem = pl.BlockSpec(memory_space=pltpu.VMEM)
    smem = pl.BlockSpec(memory_space=pltpu.SMEM)
    flops = 2 * 9 * cells * 2 * (2 * hidden * hidden + 2 * hidden * chans)
    out = pl.pallas_call(
        functools.partial(corrector_kernel, n_lon, n_lat, rows),
        out_shape=jax.ShapeDtypeStruct((chans * rows, width), F32),
        in_specs=[vmem] * 8 + [smem] * 3,
        out_specs=vmem,
        scratch_shapes=[
            pltpu.VMEM(((rows + 2) * width, 3 * hidden), BF16),
            pltpu.VMEM(((rows + 2) * width, 3 * hidden), BF16),
            pltpu.VMEM((LAYERS - 1, cells, hidden), BF16),
            pltpu.VMEM((cells, hidden), F32),
            pltpu.VMEM((cells, hidden), F32),
            pltpu.VMEM((LAYERS, 9 * hidden, hidden), BF16),
            pltpu.VMEM((9 * hidden, hidden), BF16),
            pltpu.VMEM((9 * hidden, hidden), BF16),
            pltpu.VMEM((width, hidden), F32),
            pltpu.VMEM((hidden, width), BF16),
            pltpu.VMEM((exchanges, 2, edge_rows, hidden), F32),
            pltpu.VMEM((exchanges, 2, edge_rows, hidden), F32),
            pltpu.VMEM((exchanges, 2, width, hidden), BF16),
            pltpu.VMEM((place.shape[1], width), F32),
            pltpu.VMEM((n_lat, n_lon, pair, width), BF16),
            pltpu.VMEM((n_lat, n_lon, pair, width), BF16),
            pltpu.VMEM((n_lon, n_lat, pair, width), BF16),
            pltpu.VMEM((cells, width), F32),
            pltpu.VMEM((rows, width), F32),
            pltpu.VMEM((8, width), F32),
            pltpu.SemaphoreType.DMA((exchanges, 6)),
            pltpu.SemaphoreType.DMA((exchanges, 6)),
            pltpu.SemaphoreType.DMA((n_lat,)),
            pltpu.SemaphoreType.DMA((n_lat,)),
            pltpu.SemaphoreType.DMA((n_lon,)),
            pltpu.SemaphoreType.DMA((n_lon,)),
        ],
        compiler_params=pltpu.CompilerParams(
            collective_id=0, has_side_effects=True, vmem_limit_bytes=56 * 1024 * 1024
        ),
        cost_estimate=pl.CostEstimate(flops=flops, bytes_accessed=8 * 1024 * 1024, transcendentals=0),
    )(
        state.reshape(chans * rows, width),
        w0,
        wm.reshape(wm.shape[0], 9 * hidden, hidden),
        w3,
        operator,
        values.reshape(-1, width),
        place,
        precision[None, :],
        tile,
        level,
        step,
    )
    return out.reshape(chans, rows, width)


def shards(
    state,
    noise,
    first_kernel,
    middle_kernels,
    last_kernel,
    obs_values,
    obs_holder,
    obs_tile,
    obs_operator,
    obs_precision,
    noise_level,
    step_size,
):
    block_count, obs, width = obs_values.shape
    n_lon, n_lat = lax.axis_size("lon"), lax.axis_size("lat")
    slot = obs + 2
    depth = (block_count * slot + 127) // 128 * 128
    lane = lax.broadcasted_iota(jnp.int32, (1, depth), 1)
    owner = jnp.where(lane < block_count * slot, lane % block_count, block_count)
    targets = obs_holder
    listed = lax.broadcasted_iota(jnp.int32, (block_count, 1), 0)
    mine = jnp.sum(jnp.where(owner == listed, targets, 0), axis=0, keepdims=True)
    rank = jnp.sum(
        ((targets == mine) & (listed < owner)).astype(jnp.int32), axis=0, keepdims=True
    )
    place = ((mine % n_lat) * n_lon + mine // n_lat) * CAPACITY + rank
    place = jnp.where(owner < block_count, place * slot + lane // block_count, -1)
    total = corrector(
        state,
        jnp.swapaxes(first_kernel, 1, 2),
        middle_kernels,
        last_kernel,
        obs_operator,
        jnp.swapaxes(obs_values, 0, 1),
        place,
        obs_precision,
        obs_tile,
        noise_level,
        step_size,
    )
    return state + total + jnp.sqrt(2.0 * step_size[0]) * noise


def solution(mesh):
    placed = (
        P(None, "lat", "lon"),
        P(None, "lat", "lon"),
        P(),
        P(),
        P(),
        P(("lon", "lat"), None, None),
        P(("lon", "lat"), None),
        P(("lon", "lat")),
        P(),
        P(),
        P(),
        P(),
    )
    return jax.shard_map(
        shards, mesh=mesh, in_specs=placed, out_specs=P(None, "lat", "lon"), check_vma=False
    )
```

```python
import functools

import jax
import jax.numpy as jnp
from jax import lax
from jax.experimental import pallas as pl
from jax.experimental.pallas import tpu as pltpu
from jax.sharding import PartitionSpec as P

LAYERS = 4
CAPACITY = 2
MESH = pl.DeviceIdType.MESH
F32 = jnp.float32
BF16 = jnp.bfloat16
NT = (((1,), (1,)), ((), ()))
NN = (((1,), (0,)), ((), ()))


def mm(a, b, dims):
    return lax.dot_general(a, b, dims, preferred_element_type=F32)


def rows_padded(x, rows):
    extra = rows - x.shape[0]
    return jnp.concatenate([x, jnp.zeros((extra,) + x.shape[1:], x.dtype)], axis=0)


def corrector_kernel(
    n_lon,
    n_lat,
    rows,
    state_ref,
    w0_hbm,
    wm_hbm,
    w3_hbm,
    op_ref,
    values_ref,
    place_ref,
    precision_ref,
    tile_ref,
    level_ref,
    step_ref,
    out_ref,
    xa_s,
    xb_s,
    g_s,
    state_s,
    tot_s,
    wf_s,
    w0p_s,
    w3p_s,
    opp_s,
    opt_s,
    edge_s,
    lon_s,
    lat_s,
    block_s,
    route_s,
    first_s,
    second_s,
    pv_s,
    count_s,
    precision_s,
    w0_ref,
    wm_ref,
    w3_ref,
    load_sem,
    send_sem,
    recv_sem,
    first_send,
    first_recv,
    second_send,
    second_recv,
):
    width = 128
    hidden = w0_ref.shape[2]
    chans = w0_ref.shape[1]
    obs = op_ref.shape[0]
    slot = obs + 2
    x_s = (xa_s, xb_s)
    quarter = rows // 4
    ends = [0, rows - 1]
    near = list(range(1, quarter)) + list(range(rows - quarter + 1, rows - 1))
    middle = [quarter, quarter + 1, rows - quarter - 1, rows - quarter]
    far = list(range(quarter + 2, rows - quarter - 1))
    early = [r for r in range(-1, rows + 1) if r not in far]
    early_rows = (len(early) + 7) // 8 * 8
    late_rows = (len(far) + 7) // 8 * 8

    def at_edge(row):
        return early.index(row) if row in early else early_rows + far.index(row)

    pair = first_s.shape[2]
    lon, lat = lax.axis_index("lon"), lax.axis_index("lat")
    right, left = lax.rem(lon + 1, n_lon), lax.rem(lon + n_lon - 1, n_lon)
    down, up = lax.rem(lat + 1, n_lat), lax.rem(lat + n_lat - 1, n_lat)

    loads = [
        pltpu.make_async_copy(src, dst, load_sem.at[k])
        for k, (src, dst) in enumerate(((w0_hbm, w0_ref), (wm_hbm, wm_ref), (w3_hbm, w3_ref)))
    ]
    for load in loads:
        load.start()

    barrier = pltpu.get_barrier_semaphore()
    for k in range(1, n_lat):
        where = (lon, lax.rem(lat + k, n_lat))
        pl.semaphore_signal(barrier, inc=1, device_id=where, device_id_type=MESH)
    for k in range(1, n_lon):
        where = (lax.rem(lon + k, n_lon), lat)
        pl.semaphore_signal(barrier, inc=1, device_id=where, device_id_type=MESH)
    pl.semaphore_wait(barrier, n_lat + n_lon - 2)

    def remote(src, dst, ssem, rsem, where):
        return pltpu.make_async_remote_copy(
            src_ref=src,
            dst_ref=dst,
            send_sem=ssem,
            recv_sem=rsem,
            device_id=where,
            device_id_type=MESH,
        )

    def lat_copies(e):
        x = x_s[e % 2]
        mid = pl.ds(hidden, hidden)
        return (
            remote(
                x.at[pl.ds(width, width), mid],
                lat_s.at[e, 1],
                send_sem.at[e, 0],
                recv_sem.at[e, 0],
                (lon, up),
            ),
            remote(
                x.at[pl.ds(rows * width, width), mid],
                lat_s.at[e, 0],
                send_sem.at[e, 1],
                recv_sem.at[e, 1],
                (lon, down),
            ),
        )

    def lon_copies(e, late):
        span = pl.ds(early_rows, late_rows) if late else pl.ds(0, early_rows)
        k = 4 if late else 2
        return (
            remote(
                edge_s.at[e, 1, span],
                lon_s.at[e, 0, span],
                send_sem.at[e, k],
                recv_sem.at[e, k],
                (right, lat),
            ),
            remote(
                edge_s.at[e, 0, span],
                lon_s.at[e, 1, span],
                send_sem.at[e, k + 1],
                recv_sem.at[e, k + 1],
                (left, lat),
            ),
        )

    def first_copies():
        return [
            remote(
                route_s.at[lax.rem(lat + k, n_lat)],
                first_s.at[lat],
                first_send.at[k],
                first_recv.at[k],
                (lon, lax.rem(lat + k, n_lat)),
            )
            for k in range(1, n_lat)
        ]

    def second_copies():
        return [
            remote(
                first_s.at[:, lax.rem(lon + k, n_lon)],
                second_s.at[lon],
                second_send.at[k],
                second_recv.at[k],
                (lax.rem(lon + k, n_lon), lat),
            )
            for k in range(1, n_lon)
        ]

    def part(e, q):
        return (q if e < LAYERS else 2 - q) * hidden

    def span_of(row):
        return pl.ds((row + 1) * width, width)

    halves = [pl.ds(h, width) for h in range(0, hidden, width)]

    def put_tile(e, row, h, act):
        x = x_s[e % 2]
        span = span_of(row)
        x[span, pl.ds(hidden + h * width, width)] = act.astype(BF16)
        x[span, pl.ds(part(e, 0) + h * width, width)] = pltpu.roll(act, 1, 0).astype(BF16)
        x[span, pl.ds(part(e, 2) + h * width, width)] = pltpu.roll(act, width - 1, 0).astype(BF16)
        edge_s[e, 0, pl.ds(at_edge(row), 1), halves[h]] = act[0:1, :]
        edge_s[e, 1, pl.ds(at_edge(row), 1), halves[h]] = act[width - 1 : width, :]

    def put_row(e, row, act):
        for h in range(len(halves)):
            put_tile(e, row, h, act[:, h * width : (h + 1) * width])

    def start(copies):
        for copy in copies:
            copy.start()

    def finish_lat(e):
        for copy in lat_copies(e):
            copy.wait()
        top = jnp.where(lat == 0, 0.0, 1.0).astype(F32)
        bottom = jnp.where(lat == n_lat - 1, 0.0, 1.0).astype(F32)
        put_row(e, -1, lat_s[e, 0].astype(F32) * top)
        put_row(e, rows, lat_s[e, 1].astype(F32) * bottom)

    def finish_lon(e, late):
        x = x_s[e % 2]
        for copy in lon_copies(e, late):
            copy.wait()
        first = lax.broadcasted_iota(jnp.int32, (16, hidden), 0)
        before, after = pl.ds(part(e, 0), hidden), pl.ds(part(e, 2), hidden)
        for row in far if late else early:
            spot = pl.ds(at_edge(row), 1)
            a = pl.ds((row + 1) * width, 16)
            x[a, before] = jnp.where(
                first == 0, lon_s[e, 0, spot, :], x[a, before].astype(F32)
            ).astype(BF16)
            b = pl.ds((row + 2) * width - 16, 16)
            x[b, after] = jnp.where(
                first == 15, lon_s[e, 1, spot, :], x[b, after].astype(F32)
            ).astype(BF16)

    def windows(e, group):
        order = (0, 1, 2) if e < LAYERS else (2, 1, 0)
        x = x_s[e % 2]
        return jnp.concatenate(
            [
                jnp.concatenate([x[span_of(row + p - 1), :] for row in group], axis=0)
                for p in order
            ],
            axis=1,
        )

    def layer_pass(e, body):
        sends = e + 1 < 2 * LAYERS
        finish_lon(e, False)
        body(ends)
        if sends:
            start(lat_copies(e + 1))
        body(near)
        finish_lon(e, True)
        body(middle)
        if sends:
            finish_lat(e + 1)
            start(lon_copies(e + 1, False))
        body(far)
        if sends:
            start(lon_copies(e + 1, True))

    eye = (
        lax.broadcasted_iota(jnp.int32, (hidden, hidden), 0)
        == lax.broadcasted_iota(jnp.int32, (hidden, hidden), 1)
    ).astype(F32).astype(BF16)

    edge_s[...] = jnp.zeros_like(edge_s)

    def load_row(row):
        field = state_ref[pl.ds(row, chans, stride=rows), :]
        turned = rows_padded(field, hidden).T
        state_s[pl.ds(row * width, width), :] = turned
        put_row(0, row, turned)

    for row in ends:
        load_row(row)
    start(lat_copies(0))
    for row in range(1, rows - 1):
        load_row(row)

    def tap(t):
        return pl.ds(t * hidden, hidden)

    count = tile_ref.shape[0]
    block_s[...] = jnp.zeros_like(block_s)
    block_s[0 : obs * count, :] = values_ref[...].astype(F32)

    def fill(b, carry):
        number = jnp.full((1, width), tile_ref[b] + 1, jnp.int32).astype(F32)
        block_s[pl.ds(obs * count + b, 1), :] = number
        return carry

    lax.fori_loop(0, count, fill, 0)
    block_s[(obs + 1) * count : slot * count, :] = jnp.ones((count, width), F32)
    blocks = block_s[...].astype(BF16)
    per_lat = n_lon * pair

    def route(i, carry):
        ids = lax.broadcasted_iota(jnp.int32, (per_lat, blocks.shape[0]), 0) + i * per_lat
        chosen = (ids == place_ref[...]).astype(F32).astype(BF16)
        picked = mm(chosen, blocks, NN).astype(BF16)
        for j in range(n_lon):
            route_s[i, j] = picked[j * pair : (j + 1) * pair]
        return carry

    lax.fori_loop(0, n_lat, route, 0)
    start(first_copies())
    first_s[lat] = route_s[lat]
    finish_lat(0)
    start(lon_copies(0, False))
    start(lon_copies(0, True))

    opp_s[...] = jnp.zeros_like(opp_s)
    opp_s[0:obs, 0:chans] = op_ref[...].astype(F32)
    precision_s[...] = jnp.zeros_like(precision_s)
    precision_s[0:1, 0:obs] = precision_ref[...]
    wf_s[0] = jnp.zeros_like(wf_s[0])
    for load in loads:
        load.wait()
    w3p_s[...] = jnp.zeros_like(w3p_s)
    for t in range(9):
        wf_s[0, t * hidden : t * hidden + chans, :] = w0_ref[t]
        w3p_s[t * hidden : t * hidden + chans, :] = w3_ref[t]

    def turn(dst, src):
        wide = mm(eye, src[...], NT).astype(BF16)
        for t in range(9):
            dst[tap(t), :] = wide[:, t * hidden : (t + 1) * hidden]

    def turn_ahead(layer):
        if layer == 0:
            opt_s[...] = mm(eye, opp_s[...].astype(BF16), NT).astype(BF16)
            turn(wf_s.at[1], wm_ref.at[0])
        if layer == 1:
            turn(wf_s.at[2], wm_ref.at[1])
        if layer == 2:
            turn(wf_s.at[3], w3p_s)

    def cells_of(group):
        return [pl.ds(row * width, width) for row in group]

    def pick(ref, group):
        return jnp.concatenate([ref[span, :] for span in cells_of(group)], axis=0)

    def cells(field, i):
        return field[i * width : (i + 1) * width]

    for layer in range(LAYERS - 1):
        turn_ahead(layer)
        if layer == 1:
            for copy in first_copies():
                copy.wait()
            start(second_copies())
            second_s[lon] = first_s[:, lon]

        def forward(group, layer=layer):
            pre = mm(windows(layer, group), wf_s[layer], NN)
            for i, span in enumerate(cells_of(group)):
                for h, half in enumerate(halves):
                    v = cells(pre, i)[:, h * width : (h + 1) * width]
                    s = 0.5 * jnp.tanh(0.5 * v) + 0.5
                    put_tile(layer + 1, group[i], h, v * s)
                    g_s[layer, span, half] = (s * (1.0 + v * (1.0 - s))).astype(BF16)

        layer_pass(layer, forward)

    for copy in second_copies():
        copy.wait()

    def gather(i, sums):
        both = second_s[i // n_lat, lax.rem(i, n_lat)].astype(F32)
        sums = list(sums)
        for j in range(CAPACITY):
            one = both[j * slot : (j + 1) * slot]
            ids = one[obs : obs + 1]
            for r in range(rows):
                sums[r] = sums[r] + jnp.where(ids == float(r + 1), one, 0.0)
        return tuple(sums)

    sums = lax.fori_loop(
        0, n_lon * n_lat, gather, tuple(jnp.zeros((slot, width), F32) for r in range(rows))
    )
    precision = precision_s[0:1, :]
    for r in range(rows):
        pv_s[pl.ds(r * width, width), :] = rows_padded(sums[r], width).T * precision
        count_s[r : r + 1, :] = sums[r][obs + 1 : obs + 2, :] * precision

    last = LAYERS - 1
    level = jnp.full((1, hidden), level_ref[0], F32)
    inverse = 1.0 / (level * level)

    def observe(group):
        pre = mm(windows(last, group), wf_s[last], NN)
        denoised = (pick(state_s, group) + pre).astype(BF16)
        predicted = mm(denoised, opt_s[...], NN)
        weighted = jnp.concatenate(
            [
                pv_s[span, :] - count_s[row : row + 1, :] * cells(predicted, i)
                for i, (row, span) in enumerate(zip(group, cells_of(group)))
            ],
            axis=0,
        )
        pulled = mm(weighted.astype(BF16), opp_s[...].astype(BF16), NN)
        total = pre * inverse + pulled
        for i, span in enumerate(cells_of(group)):
            tot_s[span, :] = cells(total, i)
            put_row(last + 1, group[i], cells(pulled, i))

    layer_pass(last, observe)
    turn(w0p_s, wf_s.at[0])

    for layer in range(LAYERS - 1, 0, -1):
        e = 2 * LAYERS - 1 - layer

        def backward(group, layer=layer, e=e):
            taps = w3p_s[...] if layer == LAYERS - 1 else wm_ref[layer - 1]
            back = mm(windows(e, group), taps, NN)
            for i, span in enumerate(cells_of(group)):
                for h, half in enumerate(halves):
                    cot = cells(back, i)[:, h * width : (h + 1) * width]
                    put_tile(e + 1, group[i], h, cot * g_s[layer - 1, span, half].astype(F32))

        layer_pass(e, backward)

    e = 2 * LAYERS - 1
    step = jnp.full((1, width), step_ref[0], F32)

    def finish(group):
        total = pick(tot_s, group) + mm(windows(e, group), w0p_s[...], NN)
        for i, row in enumerate(group):
            out_ref[pl.ds(row, chans, stride=rows), :] = cells(total, i).T[0:chans] * step

    layer_pass(e, finish)


def corrector(state, w0, wm, w3, operator, values, place, precision, tile, level, step):
    chans, rows, width = state.shape
    hidden = w0.shape[2]
    exchanges = 2 * LAYERS
    far = rows // 2 - 3
    edge_rows = (rows + 2 - far + 7) // 8 * 8 + (far + 7) // 8 * 8
    cells = rows * width
    slot = values.shape[0] + 2
    pair = CAPACITY * slot
    n_lon, n_lat = lax.axis_size("lon"), lax.axis_size("lat")
    vmem = pl.BlockSpec(memory_space=pltpu.VMEM)
    smem = pl.BlockSpec(memory_space=pltpu.SMEM)
    flops = 2 * 9 * cells * 2 * (2 * hidden * hidden + 2 * hidden * chans)
    out = pl.pallas_call(
        functools.partial(corrector_kernel, n_lon, n_lat, rows),
        out_shape=jax.ShapeDtypeStruct((chans * rows, width), F32),
        in_specs=[vmem] + [pl.BlockSpec(memory_space=pl.ANY)] * 3 + [vmem] * 4 + [smem] * 3,
        out_specs=vmem,
        scratch_shapes=[
            pltpu.VMEM(((rows + 2) * width, 3 * hidden), BF16),
            pltpu.VMEM(((rows + 2) * width, 3 * hidden), BF16),
            pltpu.VMEM((LAYERS - 1, cells, hidden), BF16),
            pltpu.VMEM((cells, hidden), F32),
            pltpu.VMEM((cells, hidden), F32),
            pltpu.VMEM((LAYERS, 9 * hidden, hidden), BF16),
            pltpu.VMEM((9 * hidden, hidden), BF16),
            pltpu.VMEM((9 * hidden, hidden), BF16),
            pltpu.VMEM((width, hidden), F32),
            pltpu.VMEM((hidden, width), BF16),
            pltpu.VMEM((exchanges, 2, edge_rows, hidden), F32),
            pltpu.VMEM((exchanges, 2, edge_rows, hidden), F32),
            pltpu.VMEM((exchanges, 2, width, hidden), BF16),
            pltpu.VMEM((place.shape[1], width), F32),
            pltpu.VMEM((n_lat, n_lon, pair, width), BF16),
            pltpu.VMEM((n_lat, n_lon, pair, width), BF16),
            pltpu.VMEM((n_lon, n_lat, pair, width), BF16),
            pltpu.VMEM((cells, width), F32),
            pltpu.VMEM((rows, width), F32),
            pltpu.VMEM((8, width), F32),
            pltpu.VMEM(w0.shape, BF16),
            pltpu.VMEM((wm.shape[0], 9 * hidden, hidden), BF16),
            pltpu.VMEM(w3.shape, BF16),
            pltpu.SemaphoreType.DMA((3,)),
            pltpu.SemaphoreType.DMA((exchanges, 6)),
            pltpu.SemaphoreType.DMA((exchanges, 6)),
            pltpu.SemaphoreType.DMA((n_lat,)),
            pltpu.SemaphoreType.DMA((n_lat,)),
            pltpu.SemaphoreType.DMA((n_lon,)),
            pltpu.SemaphoreType.DMA((n_lon,)),
        ],
        compiler_params=pltpu.CompilerParams(
            collective_id=0, has_side_effects=True, vmem_limit_bytes=56 * 1024 * 1024
        ),
        cost_estimate=pl.CostEstimate(flops=flops, bytes_accessed=8 * 1024 * 1024, transcendentals=0),
    )(
        state.reshape(chans * rows, width),
        w0,
        wm.reshape(wm.shape[0], 9 * hidden, hidden),
        w3,
        operator,
        values.reshape(-1, width),
        place,
        precision[None, :],
        tile,
        level,
        step,
    )
    return out.reshape(chans, rows, width)


def shards(
    state,
    noise,
    first_kernel,
    middle_kernels,
    last_kernel,
    obs_values,
    obs_holder,
    obs_tile,
    obs_operator,
    obs_precision,
    noise_level,
    step_size,
):
    block_count, obs, width = obs_values.shape
    n_lon, n_lat = lax.axis_size("lon"), lax.axis_size("lat")
    slot = obs + 2
    depth = (block_count * slot + 127) // 128 * 128
    lane = lax.broadcasted_iota(jnp.int32, (1, depth), 1)
    owner = jnp.where(lane < block_count * slot, lane % block_count, block_count)
    targets = obs_holder
    listed = lax.broadcasted_iota(jnp.int32, (block_count, 1), 0)
    mine = jnp.sum(jnp.where(owner == listed, targets, 0), axis=0, keepdims=True)
    rank = jnp.sum(
        ((targets == mine) & (listed < owner)).astype(jnp.int32), axis=0, keepdims=True
    )
    place = ((mine % n_lat) * n_lon + mine // n_lat) * CAPACITY + rank
    place = jnp.where(owner < block_count, place * slot + lane // block_count, -1)
    total = corrector(
        state,
        jnp.swapaxes(first_kernel, 1, 2),
        middle_kernels,
        last_kernel,
        obs_operator,
        jnp.swapaxes(obs_values, 0, 1),
        place,
        obs_precision,
        obs_tile,
        noise_level,
        step_size,
    )
    return state + total + jnp.sqrt(2.0 * step_size[0]) * noise


def solution(mesh):
    placed = (
        P(None, "lat", "lon"),
        P(None, "lat", "lon"),
        P(),
        P(),
        P(),
        P(("lon", "lat"), None, None),
        P(("lon", "lat"), None),
        P(("lon", "lat")),
        P(),
        P(),
        P(),
        P(),
    )
    return jax.shard_map(
        shards, mesh=mesh, in_specs=placed, out_specs=P(None, "lat", "lon"), check_vma=False
    )
```

```python
import functools

import jax
import jax.numpy as jnp
from jax import lax
from jax.experimental import pallas as pl
from jax.experimental.pallas import tpu as pltpu
from jax.sharding import PartitionSpec as P

LAYERS = 4
CAPACITY = 2
MESH = pl.DeviceIdType.MESH
F32 = jnp.float32
BF16 = jnp.bfloat16
NT = (((1,), (1,)), ((), ()))
NN = (((1,), (0,)), ((), ()))


def mm(a, b, dims):
    return lax.dot_general(a, b, dims, preferred_element_type=F32)


def rows_padded(x, rows):
    extra = rows - x.shape[0]
    return jnp.concatenate([x, jnp.zeros((extra,) + x.shape[1:], x.dtype)], axis=0)


def corrector_kernel(
    n_lon,
    n_lat,
    rows,
    state_ref,
    w0_hbm,
    wm_hbm,
    w3_hbm,
    op_ref,
    values_ref,
    place_ref,
    precision_ref,
    tile_ref,
    level_ref,
    step_ref,
    out_ref,
    xa_s,
    xb_s,
    g_s,
    state_s,
    tot_s,
    wf_s,
    w0p_s,
    w3p_s,
    opp_s,
    opt_s,
    edge_s,
    lon_s,
    lat_s,
    block_s,
    route_s,
    first_s,
    second_s,
    pv_s,
    count_s,
    precision_s,
    w0_ref,
    wm_ref,
    w3_ref,
    wmb_s,
    z_s,
    load_sem,
    send_sem,
    recv_sem,
    first_send,
    first_recv,
    second_send,
    second_recv,
):
    width = 128
    hidden = w0_ref.shape[2]
    chans = w0_ref.shape[1]
    obs = op_ref.shape[0]
    slot = obs + 2
    x_s = (xa_s, xb_s)
    quarter = rows // 4
    ends = [0, rows - 1]
    near = list(range(1, quarter)) + list(range(rows - quarter + 1, rows - 1))
    middle = [quarter, quarter + 1, rows - quarter - 1, rows - quarter]
    far = list(range(quarter + 2, rows - quarter - 1))
    early = [r for r in range(-1, rows + 1) if r not in far]
    early_rows = (len(early) + 7) // 8 * 8
    late_rows = (len(far) + 7) // 8 * 8

    def at_edge(row):
        return early.index(row) if row in early else early_rows + far.index(row)

    pair = first_s.shape[2]
    lon, lat = lax.axis_index("lon"), lax.axis_index("lat")
    right, left = lax.rem(lon + 1, n_lon), lax.rem(lon + n_lon - 1, n_lon)
    down, up = lax.rem(lat + 1, n_lat), lax.rem(lat + n_lat - 1, n_lat)

    loads = [
        pltpu.make_async_copy(src, dst, load_sem.at[k])
        for k, (src, dst) in enumerate(((w0_hbm, w0_ref), (wm_hbm, wm_ref), (w3_hbm, w3_ref)))
    ]
    for load in loads:
        load.start()

    barrier = pltpu.get_barrier_semaphore()
    for k in range(1, n_lat):
        where = (lon, lax.rem(lat + k, n_lat))
        pl.semaphore_signal(barrier, inc=1, device_id=where, device_id_type=MESH)
    for k in range(1, n_lon):
        where = (lax.rem(lon + k, n_lon), lat)
        pl.semaphore_signal(barrier, inc=1, device_id=where, device_id_type=MESH)
    pl.semaphore_wait(barrier, n_lat + n_lon - 2)

    def remote(src, dst, ssem, rsem, where):
        return pltpu.make_async_remote_copy(
            src_ref=src,
            dst_ref=dst,
            send_sem=ssem,
            recv_sem=rsem,
            device_id=where,
            device_id_type=MESH,
        )

    def lat_copies(e):
        x = x_s[e % 2]
        mid = pl.ds(hidden, hidden)
        return (
            remote(
                x.at[pl.ds(width, width), mid],
                lat_s.at[e, 1],
                send_sem.at[e, 0],
                recv_sem.at[e, 0],
                (lon, up),
            ),
            remote(
                x.at[pl.ds(rows * width, width), mid],
                lat_s.at[e, 0],
                send_sem.at[e, 1],
                recv_sem.at[e, 1],
                (lon, down),
            ),
        )

    def lon_copies(e, late):
        span = pl.ds(early_rows, late_rows) if late else pl.ds(0, early_rows)
        k = 4 if late else 2
        return (
            remote(
                edge_s.at[e, 1, span],
                lon_s.at[e, 0, span],
                send_sem.at[e, k],
                recv_sem.at[e, k],
                (right, lat),
            ),
            remote(
                edge_s.at[e, 0, span],
                lon_s.at[e, 1, span],
                send_sem.at[e, k + 1],
                recv_sem.at[e, k + 1],
                (left, lat),
            ),
        )

    def first_copies():
        return [
            remote(
                route_s.at[lax.rem(lat + k, n_lat)],
                first_s.at[lat],
                first_send.at[k],
                first_recv.at[k],
                (lon, lax.rem(lat + k, n_lat)),
            )
            for k in range(1, n_lat)
        ]

    def second_copies():
        return [
            remote(
                first_s.at[:, lax.rem(lon + k, n_lon)],
                second_s.at[lon],
                second_send.at[k],
                second_recv.at[k],
                (lax.rem(lon + k, n_lon), lat),
            )
            for k in range(1, n_lon)
        ]

    def part(e, q):
        return (q if e < LAYERS else 2 - q) * hidden

    def span_of(row):
        return pl.ds((row + 1) * width, width)

    halves = [pl.ds(h, width) for h in range(0, hidden, width)]

    def put_tile(e, row, h, act):
        x = x_s[e % 2]
        span = span_of(row)
        x[span, pl.ds(hidden + h * width, width)] = act.astype(BF16)
        x[span, pl.ds(part(e, 0) + h * width, width)] = pltpu.roll(act, 1, 0).astype(BF16)
        x[span, pl.ds(part(e, 2) + h * width, width)] = pltpu.roll(act, width - 1, 0).astype(BF16)
        edge_s[e, 0, pl.ds(at_edge(row), 1), halves[h]] = act[0:1, :]
        edge_s[e, 1, pl.ds(at_edge(row), 1), halves[h]] = act[width - 1 : width, :]

    def put_row(e, row, act):
        for h in range(len(halves)):
            put_tile(e, row, h, act[:, h * width : (h + 1) * width])

    def start(copies):
        for copy in copies:
            copy.start()

    def finish_lat(e):
        for copy in lat_copies(e):
            copy.wait()
        top = jnp.where(lat == 0, 0.0, 1.0).astype(F32)
        bottom = jnp.where(lat == n_lat - 1, 0.0, 1.0).astype(F32)
        put_row(e, -1, lat_s[e, 0].astype(F32) * top)
        put_row(e, rows, lat_s[e, 1].astype(F32) * bottom)

    def finish_lon(e, late):
        x = x_s[e % 2]
        for copy in lon_copies(e, late):
            copy.wait()
        first = lax.broadcasted_iota(jnp.int32, (16, hidden), 0)
        before, after = pl.ds(part(e, 0), hidden), pl.ds(part(e, 2), hidden)
        for row in far if late else early:
            spot = pl.ds(at_edge(row), 1)
            a = pl.ds((row + 1) * width, 16)
            x[a, before] = jnp.where(
                first == 0, lon_s[e, 0, spot, :], x[a, before].astype(F32)
            ).astype(BF16)
            b = pl.ds((row + 2) * width - 16, 16)
            x[b, after] = jnp.where(
                first == 15, lon_s[e, 1, spot, :], x[b, after].astype(F32)
            ).astype(BF16)

    def products(e, fields, taps):
        x = x_s[e % 2]
        z = mm(jnp.concatenate([x[span_of(row), :] for row in fields], axis=0), taps, NN)
        for i, row in enumerate(fields):
            z_s[span_of(row), :] = z[i * width : (i + 1) * width]

    def summed(e, row, first, size):
        order = (0, 1, 2) if e < LAYERS else (2, 1, 0)
        terms = [
            z_s[span_of(row + p - 1), pl.ds(k * hidden + first, size)] for k, p in enumerate(order)
        ]
        return terms[0] + terms[1] + terms[2]

    def convolved(e, group):
        return jnp.concatenate([summed(e, row, 0, hidden) for row in group], axis=0)

    def layer_pass(e, taps, body):
        sends = e + 1 < 2 * LAYERS
        finish_lon(e, False)
        products(e, [-1, 0, 1, rows - 2, rows - 1, rows], taps())
        body(ends)
        if sends:
            start(lat_copies(e + 1))
        low, high = quarter, rows - quarter
        products(e, list(range(2, low + 1)) + list(range(high, rows - 2)), taps())
        body(near)
        finish_lon(e, True)
        products(e, [low + 1, low + 2, high - 2, high - 1], taps())
        body(middle)
        if sends:
            finish_lat(e + 1)
            start(lon_copies(e + 1, False))
        products(e, list(range(low + 3, high - 2)), taps())
        body(far)
        if sends:
            start(lon_copies(e + 1, True))

    eye = (
        lax.broadcasted_iota(jnp.int32, (hidden, hidden), 0)
        == lax.broadcasted_iota(jnp.int32, (hidden, hidden), 1)
    ).astype(F32).astype(BF16)

    edge_s[...] = jnp.zeros_like(edge_s)

    def load_row(row):
        field = state_ref[pl.ds(row, chans, stride=rows), :]
        turned = rows_padded(field, hidden).T
        state_s[pl.ds(row * width, width), :] = turned
        put_row(0, row, turned)

    for row in ends:
        load_row(row)
    start(lat_copies(0))
    for row in range(1, rows - 1):
        load_row(row)

    def tile(t, size=hidden):
        return pl.ds(t % 3 * hidden, size), pl.ds(t // 3 * hidden, hidden)

    count = tile_ref.shape[0]
    block_s[...] = jnp.zeros_like(block_s)
    block_s[0 : obs * count, :] = values_ref[...].astype(F32)

    def fill(b, carry):
        number = jnp.full((1, width), tile_ref[b] + 1, jnp.int32).astype(F32)
        block_s[pl.ds(obs * count + b, 1), :] = number
        return carry

    lax.fori_loop(0, count, fill, 0)
    block_s[(obs + 1) * count : slot * count, :] = jnp.ones((count, width), F32)
    blocks = block_s[...].astype(BF16)
    per_lat = n_lon * pair

    def route(i, carry):
        ids = lax.broadcasted_iota(jnp.int32, (per_lat, blocks.shape[0]), 0) + i * per_lat
        chosen = (ids == place_ref[...]).astype(F32).astype(BF16)
        picked = mm(chosen, blocks, NN).astype(BF16)
        for j in range(n_lon):
            route_s[i, j] = picked[j * pair : (j + 1) * pair]
        return carry

    lax.fori_loop(0, n_lat, route, 0)
    start(first_copies())
    first_s[lat] = route_s[lat]
    finish_lat(0)
    start(lon_copies(0, False))
    start(lon_copies(0, True))

    opp_s[...] = jnp.zeros_like(opp_s)
    opp_s[0:obs, 0:chans] = op_ref[...].astype(F32)
    precision_s[...] = jnp.zeros_like(precision_s)
    precision_s[0:1, 0:obs] = precision_ref[...]
    wf_s[0] = jnp.zeros_like(wf_s[0])
    for load in loads:
        load.wait()
    w3p_s[...] = jnp.zeros_like(w3p_s)
    for t in range(9):
        wf_s[(0,) + tile(t, chans)] = w0_ref[t]
        w3p_s[tile(t, chans)] = w3_ref[t]
        for m in range(LAYERS - 2):
            wmb_s[(m,) + tile(t)] = wm_ref[m, t * hidden : (t + 1) * hidden, :]

    def turn(dst, src):
        for t in range(9):
            dst[tile(t)] = mm(eye, src[tile(t)], NT).astype(BF16)

    def turn_ahead(layer):
        if layer == 0:
            opt_s[...] = mm(eye, opp_s[...].astype(BF16), NT).astype(BF16)
            turn(wf_s.at[1], wmb_s.at[0])
        if layer == 1:
            turn(wf_s.at[2], wmb_s.at[1])
        if layer == 2:
            turn(wf_s.at[3], w3p_s)

    def cells_of(group):
        return [pl.ds(row * width, width) for row in group]

    def pick(ref, group):
        return jnp.concatenate([ref[span, :] for span in cells_of(group)], axis=0)

    def cells(field, i):
        return field[i * width : (i + 1) * width]

    for layer in range(LAYERS - 1):
        turn_ahead(layer)
        if layer == 1:
            for copy in first_copies():
                copy.wait()
            start(second_copies())
            second_s[lon] = first_s[:, lon]

        def forward(group, layer=layer):
            for i, span in enumerate(cells_of(group)):
                for h, half in enumerate(halves):
                    v = summed(layer, group[i], h * width, width)
                    s = 0.5 * jnp.tanh(0.5 * v) + 0.5
                    put_tile(layer + 1, group[i], h, v * s)
                    g_s[layer, span, half] = (s * (1.0 + v * (1.0 - s))).astype(BF16)

        layer_pass(layer, lambda layer=layer: wf_s[layer], forward)

    for copy in second_copies():
        copy.wait()

    def gather(i, sums):
        both = second_s[i // n_lat, lax.rem(i, n_lat)].astype(F32)
        sums = list(sums)
        for j in range(CAPACITY):
            one = both[j * slot : (j + 1) * slot]
            ids = one[obs : obs + 1]
            for r in range(rows):
                sums[r] = sums[r] + jnp.where(ids == float(r + 1), one, 0.0)
        return tuple(sums)

    sums = lax.fori_loop(
        0, n_lon * n_lat, gather, tuple(jnp.zeros((slot, width), F32) for r in range(rows))
    )
    precision = precision_s[0:1, :]
    for r in range(rows):
        pv_s[pl.ds(r * width, width), :] = rows_padded(sums[r], width).T * precision
        count_s[r : r + 1, :] = sums[r][obs + 1 : obs + 2, :] * precision

    last = LAYERS - 1
    level = jnp.full((1, hidden), level_ref[0], F32)
    inverse = 1.0 / (level * level)

    def observe(group):
        pre = convolved(last, group)
        denoised = (pick(state_s, group) + pre).astype(BF16)
        predicted = mm(denoised, opt_s[...], NN)
        weighted = jnp.concatenate(
            [
                pv_s[span, :] - count_s[row : row + 1, :] * cells(predicted, i)
                for i, (row, span) in enumerate(zip(group, cells_of(group)))
            ],
            axis=0,
        )
        pulled = mm(weighted.astype(BF16), opp_s[...].astype(BF16), NN)
        total = pre * inverse + pulled
        for i, span in enumerate(cells_of(group)):
            tot_s[span, :] = cells(total, i)
            put_row(last + 1, group[i], cells(pulled, i))

    layer_pass(last, lambda: wf_s[last], observe)
    turn(w0p_s, wf_s.at[0])

    for layer in range(LAYERS - 1, 0, -1):
        e = 2 * LAYERS - 1 - layer

        def backward(group, layer=layer, e=e):
            for i, span in enumerate(cells_of(group)):
                for h, half in enumerate(halves):
                    cot = summed(e, group[i], h * width, width)
                    put_tile(e + 1, group[i], h, cot * g_s[layer - 1, span, half].astype(F32))

        taps = (lambda: w3p_s[...]) if layer == LAYERS - 1 else (lambda m=layer - 1: wmb_s[m])
        layer_pass(e, taps, backward)

    e = 2 * LAYERS - 1
    step = jnp.full((1, width), step_ref[0], F32)

    def finish(group):
        total = pick(tot_s, group) + convolved(e, group)
        for i, row in enumerate(group):
            out_ref[pl.ds(row, chans, stride=rows), :] = cells(total, i).T[0:chans] * step

    layer_pass(e, lambda: w0p_s[...], finish)


def corrector(state, w0, wm, w3, operator, values, place, precision, tile, level, step):
    chans, rows, width = state.shape
    hidden = w0.shape[2]
    exchanges = 2 * LAYERS
    far = rows // 2 - 3
    edge_rows = (rows + 2 - far + 7) // 8 * 8 + (far + 7) // 8 * 8
    cells = rows * width
    slot = values.shape[0] + 2
    pair = CAPACITY * slot
    n_lon, n_lat = lax.axis_size("lon"), lax.axis_size("lat")
    vmem = pl.BlockSpec(memory_space=pltpu.VMEM)
    smem = pl.BlockSpec(memory_space=pltpu.SMEM)
    flops = 2 * 9 * cells * 2 * (2 * hidden * hidden + 2 * hidden * chans)
    out = pl.pallas_call(
        functools.partial(corrector_kernel, n_lon, n_lat, rows),
        out_shape=jax.ShapeDtypeStruct((chans * rows, width), F32),
        in_specs=[vmem] + [pl.BlockSpec(memory_space=pl.ANY)] * 3 + [vmem] * 4 + [smem] * 3,
        out_specs=vmem,
        scratch_shapes=[
            pltpu.VMEM(((rows + 2) * width, 3 * hidden), BF16),
            pltpu.VMEM(((rows + 2) * width, 3 * hidden), BF16),
            pltpu.VMEM((LAYERS - 1, cells, hidden), BF16),
            pltpu.VMEM((cells, hidden), F32),
            pltpu.VMEM((cells, hidden), F32),
            pltpu.VMEM((LAYERS, 3 * hidden, 3 * hidden), BF16),
            pltpu.VMEM((3 * hidden, 3 * hidden), BF16),
            pltpu.VMEM((3 * hidden, 3 * hidden), BF16),
            pltpu.VMEM((width, hidden), F32),
            pltpu.VMEM((hidden, width), BF16),
            pltpu.VMEM((exchanges, 2, edge_rows, hidden), F32),
            pltpu.VMEM((exchanges, 2, edge_rows, hidden), F32),
            pltpu.VMEM((exchanges, 2, width, hidden), BF16),
            pltpu.VMEM((place.shape[1], width), F32),
            pltpu.VMEM((n_lat, n_lon, pair, width), BF16),
            pltpu.VMEM((n_lat, n_lon, pair, width), BF16),
            pltpu.VMEM((n_lon, n_lat, pair, width), BF16),
            pltpu.VMEM((cells, width), F32),
            pltpu.VMEM((rows, width), F32),
            pltpu.VMEM((8, width), F32),
            pltpu.VMEM(w0.shape, BF16),
            pltpu.VMEM((wm.shape[0], 9 * hidden, hidden), BF16),
            pltpu.VMEM(w3.shape, BF16),
            pltpu.VMEM((wm.shape[0], 3 * hidden, 3 * hidden), BF16),
            pltpu.VMEM(((rows + 2) * width, 3 * hidden), F32),
            pltpu.SemaphoreType.DMA((3,)),
            pltpu.SemaphoreType.DMA((exchanges, 6)),
            pltpu.SemaphoreType.DMA((exchanges, 6)),
            pltpu.SemaphoreType.DMA((n_lat,)),
            pltpu.SemaphoreType.DMA((n_lat,)),
            pltpu.SemaphoreType.DMA((n_lon,)),
            pltpu.SemaphoreType.DMA((n_lon,)),
        ],
        compiler_params=pltpu.CompilerParams(
            collective_id=0, has_side_effects=True, vmem_limit_bytes=56 * 1024 * 1024
        ),
        cost_estimate=pl.CostEstimate(flops=flops, bytes_accessed=8 * 1024 * 1024, transcendentals=0),
    )(
        state.reshape(chans * rows, width),
        w0,
        wm.reshape(wm.shape[0], 9 * hidden, hidden),
        w3,
        operator,
        values.reshape(-1, width),
        place,
        precision[None, :],
        tile,
        level,
        step,
    )
    return out.reshape(chans, rows, width)


def shards(
    state,
    noise,
    first_kernel,
    middle_kernels,
    last_kernel,
    obs_values,
    obs_holder,
    obs_tile,
    obs_operator,
    obs_precision,
    noise_level,
    step_size,
):
    block_count, obs, width = obs_values.shape
    n_lon, n_lat = lax.axis_size("lon"), lax.axis_size("lat")
    slot = obs + 2
    depth = (block_count * slot + 127) // 128 * 128
    lane = lax.broadcasted_iota(jnp.int32, (1, depth), 1)
    owner = jnp.where(lane < block_count * slot, lane % block_count, block_count)
    targets = obs_holder
    listed = lax.broadcasted_iota(jnp.int32, (block_count, 1), 0)
    mine = jnp.sum(jnp.where(owner == listed, targets, 0), axis=0, keepdims=True)
    rank = jnp.sum(
        ((targets == mine) & (listed < owner)).astype(jnp.int32), axis=0, keepdims=True
    )
    place = ((mine % n_lat) * n_lon + mine // n_lat) * CAPACITY + rank
    place = jnp.where(owner < block_count, place * slot + lane // block_count, -1)
    total = corrector(
        state,
        jnp.swapaxes(first_kernel, 1, 2),
        middle_kernels,
        last_kernel,
        obs_operator,
        jnp.swapaxes(obs_values, 0, 1),
        place,
        obs_precision,
        obs_tile,
        noise_level,
        step_size,
    )
    return state + total + jnp.sqrt(2.0 * step_size[0]) * noise


def solution(mesh):
    placed = (
        P(None, "lat", "lon"),
        P(None, "lat", "lon"),
        P(),
        P(),
        P(),
        P(("lon", "lat"), None, None),
        P(("lon", "lat"), None),
        P(("lon", "lat")),
        P(),
        P(),
        P(),
        P(),
    )
    return jax.shard_map(
        shards, mesh=mesh, in_specs=placed, out_specs=P(None, "lat", "lon"), check_vma=False
    )
```
